128 devices in a mesh: blocks: 128 (over y, z, x, core).
Axes of the slice: x: 4, y: 4, z: 4, core: 2. Of those that a mesh axis runs over, the one named last changes fastest.
Arguments:
- pdfs: float32 [512, 19, 4096], P('blocks'), may hold values from 0.25 to 21, as said below
- plan: int32 [512], P('blocks'), may hold values from 0 to 511, as said below
- neighbours: int32 [512, 6], P('blocks'), may hold values from -1 to 511, as said below
- flags: int32 [512, 4096], P('blocks'), may hold values 0 or 1
Outputs:
- final_pdfs: float32 [512, 19, 4096], P('blocks')
The draws below stay inside these ranges and needn't reach their ends.
Inputs may be any that keep to these rules, and one draw needn't show every extreme that they name: `plan`: A permutation of the places. Each device sends exactly 1 block to each of 4 owners, which lie at distinct offsets from -2 to 2 around the cycle of devices; the offsets are the same for every device, and an owner keeps the received blocks in an order of offset that is the same for every owner. `neighbours`: Symmetric: if the block across the upper face of b along an axis is n, the block across the lower face of n along that axis is b. A neighbour's owner lies within 2 devices of the block's owner around the cycle, never the block itself; for every offset from 1 to 2 in either direction, exactly 6 faces of one device's blocks border blocks of the device at that offset. `pdfs`: positive populations near a rest state.
All inputs are finite; a program needn't handle non-finite values. No bound on the sum of `flags` on one device may be relied on, other than what follows from the above.
Results may differ from the reference program's by a relative error of at most 0.0001.
Values sent between devices are 32-bit elements; how exact they have to be, the bound alone decides.
No kernel may reach another device: no remote copies, remote signals or barrier semaphores. Data moves between devices by JAX's collectives and lax.ppermute only.
A program may use at most 192 MiB of HBM per device.

```python
import jax
import jax.numpy as jnp
import numpy as np
from jax import lax

EDGE = 16
BLK_DEV = 4
GROUPS = 4
REACH = 2
LINKS = 1
STEPS = 3
CAP = 1
NBLK = 512
N_BLOCKS = 128


def draw_pdfs(key, part):
    weights = jnp.asarray(np.array([1.0 / 3.0] + [1.0 / 18.0] * 6 + [1.0 / 36.0] * 12), jnp.float32)
    cells = EDGE ** 3
    noise = jnp.clip(jax.random.normal(jax.random.fold_in(key, 1), (NBLK, 19, cells), jnp.float32), -3.0, 3.0)
    base = 1.0 + 0.25 * noise
    return 36.0 * weights[None, :, None] * base


def draw_plan(key, part):
    cycle = N_BLOCKS
    offsets = jax.random.permutation(jax.random.fold_in(key, 11), 2 * REACH + 1)[:GROUPS] - REACH
    subkeys = jax.random.split(jax.random.fold_in(key, 12), cycle)
    orders = jax.vmap(lambda subkey: jax.random.permutation(subkey, BLK_DEV))(subkeys)
    position = jnp.arange(BLK_DEV)
    group_id = position // CAP
    within = position % CAP
    device = jnp.arange(cycle)[:, None]
    owner = (device + offsets[group_id][None, :]) % cycle
    places = owner * BLK_DEV + (group_id * CAP + within)[None, :]
    result = jnp.zeros((cycle, BLK_DEV), jnp.int32).at[device, orders].set(places.astype(jnp.int32))
    return result.reshape(-1).astype(jnp.int32)


def draw_neighbours(key, part):
    cycle = N_BLOCKS
    total = cycle * BLK_DEV
    base_list = [0] * BLK_DEV
    filled = 0
    for reach_id in range(1, REACH + 1):
        for link_id in range(LINKS):
            base_list[filled] = reach_id
            base_list[filled + 1] = -reach_id
            filled = filled + 2
    base = jnp.asarray(np.array(base_list), jnp.int32)
    block_ids = jnp.arange(total)
    device = block_ids // BLK_DEV
    slot_ids = block_ids % BLK_DEV
    lower_list = []
    upper_list = []
    for axis_id in range(3):
        subkey = jax.random.fold_in(key, 20 + axis_id)
        delta = base[jax.random.permutation(jax.random.fold_in(subkey, 1), BLK_DEV)]
        mixing = jax.random.permutation(jax.random.fold_in(subkey, 2), BLK_DEV)
        partner = (device + delta[slot_ids]) % cycle * BLK_DEV + mixing[slot_ids]
        coins = jax.random.randint(jax.random.fold_in(subkey, 3), (total,), 0, 2)
        keeping = ((delta[slot_ids] != 0) | (coins == 1)) & (partner != block_ids)
        upper = jnp.where(keeping, partner, -1)
        lower = jnp.full((total,), -1, jnp.int32).at[partner].set(jnp.where(keeping, block_ids, -1).astype(jnp.int32))
        lower_list.append(lower.astype(jnp.int32))
        upper_list.append(upper.astype(jnp.int32))
    return jnp.stack([lower_list[0], upper_list[0], lower_list[1], upper_list[1], lower_list[2], upper_list[2]], axis=1).astype(jnp.int32)


def plant(drawn, rng, least, top_value):
    longest = drawn.shape.index(max(drawn.shape))
    spots = []
    for shift in (0, 1):
        where = [jax.random.randint(jax.random.fold_in(rng, axis), (), 0, length) for axis, length in enumerate(drawn.shape)]
        where[longest] = (where[longest] + shift) % drawn.shape[longest]
        spots.append(tuple(where))
    return drawn.at[spots[0]].set(least).at[spots[1]].set(top_value)


def setup_inputs(seed: int = 0) -> dict:
    streams_of = jax.random.split(jax.random.key(seed), 5)
    return {
        "pdfs": draw_pdfs(jax.random.fold_in(streams_of[4], 71), 0),
        "plan": draw_plan(jax.random.fold_in(streams_of[4], 71), 0),
        "neighbours": draw_neighbours(jax.random.fold_in(streams_of[4], 71), 0),
        "flags": plant((jax.random.randint(streams_of[3], (NBLK, EDGE**3), 0, 4) < 3).astype(jnp.int32), jax.random.fold_in(streams_of[3], 1), 0, 1),
    }


VELOCITY_TABLE = np.array([[0, 0, 0], [1, 0, 0], [-1, 0, 0], [0, 1, 0], [0, -1, 0], [0, 0, 1], [0, 0, -1],
                           [1, 1, 0], [-1, -1, 0], [1, -1, 0], [-1, 1, 0], [1, 0, 1], [-1, 0, -1], [1, 0, -1],
                           [-1, 0, 1], [0, 1, 1], [0, -1, -1], [0, 1, -1], [0, -1, 1]], np.int32)
WEIGHT_TABLE = np.array([1.0 / 3.0] + [1.0 / 18.0] * 6 + [1.0 / 36.0] * 12)
REST_DENSITY = 36.0
SHEAR_RATE = 1.6
FACE_FLIP = np.array([1, 0, 3, 2, 5, 4], np.int32)


def opposite_table():
    result = []
    for pop_id in range(19):
        same = np.all(VELOCITY_TABLE == -VELOCITY_TABLE[pop_id][None, :], axis=1)
        result.append(int(np.argmax(same)))
    return np.array(result, np.int32)


def collision_matrix():
    speeds = VELOCITY_TABLE * 1.0
    along_x, along_y, along_z = speeds[:, 0], speeds[:, 1], speeds[:, 2]
    squared = along_x * along_x + along_y * along_y + along_z * along_z
    rows = [np.ones(19), 19 * squared - 30, (21 * squared * squared - 53 * squared + 24) / 2,
            along_x, (5 * squared - 9) * along_x, along_y, (5 * squared - 9) * along_y,
            along_z, (5 * squared - 9) * along_z, 3 * along_x * along_x - squared,
            (3 * squared - 5) * (3 * along_x * along_x - squared), along_y * along_y - along_z * along_z,
            (3 * squared - 5) * (along_y * along_y - along_z * along_z), along_x * along_y,
            along_y * along_z, along_x * along_z, along_x * (along_y * along_y - along_z * along_z),
            along_y * (along_z * along_z - along_x * along_x), along_z * (along_x * along_x - along_y * along_y)]
    moments = np.stack(rows)
    rates = np.array([0, 1.19, 1.4, 0, 1.2, 0, 1.2, 0, 1.2, SHEAR_RATE, 1.4, SHEAR_RATE, 1.4,
                      SHEAR_RATE, SHEAR_RATE, SHEAR_RATE, 1.98, 1.98, 1.98])
    norms = np.sum(moments * moments, axis=1)
    return (moments.T * (rates / norms)[None, :]) @ moments


def face_tables(edge):
    face_pops = np.zeros((6, 5), np.int32)
    face_cells = np.zeros((6, edge * edge), np.int32)
    grid_u, grid_v = np.meshgrid(np.arange(edge), np.arange(edge), indexing="ij")
    for face_id in range(6):
        axis_id = face_id // 2
        side_sign = 1 if face_id % 2 else -1
        face_pops[face_id] = [pop_id for pop_id in range(19) if int(VELOCITY_TABLE[pop_id][axis_id]) == side_sign]
        others = [other for other in range(3) if other != axis_id]
        points = np.zeros((3, edge, edge), np.int32)
        points[axis_id] = edge - 1 if side_sign > 0 else 0
        points[others[0]] = grid_u
        points[others[1]] = grid_v
        face_cells[face_id] = (points[0] * edge * edge + points[1] * edge + points[2]).reshape(-1)
    return face_pops, face_cells


def stream_tables(edge):
    cells = edge ** 3
    opposite = opposite_table()
    face_pops, face_cells = face_tables(edge)
    flat_cells = np.arange(cells, dtype=np.int32)
    coords = np.stack([flat_cells // (edge * edge), (flat_cells // edge) % edge, flat_cells % edge])
    source_list = []
    ghost_list = []
    bounce_list = []
    for pop_id in range(19):
        anchor = coords - VELOCITY_TABLE[pop_id][:, None]
        outside = (anchor < 0) | (anchor >= edge)
        crossings = outside.sum(axis=0)
        bounce_idx = opposite[pop_id] * cells + flat_cells
        inner_idx = pop_id * cells + anchor[0] * edge * edge + anchor[1] * edge + anchor[2]
        source_idx = np.where(crossings == 0, inner_idx, bounce_idx)
        ghost_face = -np.ones(cells, np.int32)
        for axis_id in range(3):
            speed_part = int(VELOCITY_TABLE[pop_id][axis_id])
            if speed_part == 0:
                continue
            face_id = 2 * axis_id if speed_part > 0 else 2 * axis_id + 1
            pop_pos = int(np.argmax(face_pops[face_id ^ 1] == pop_id))
            others = [other for other in range(3) if other != axis_id]
            single = (crossings == 1) & outside[axis_id]
            ghost_idx = (19 * cells + face_id * 5 * edge * edge + pop_pos * edge * edge
                         + anchor[others[0]] * edge + anchor[others[1]])
            source_idx = np.where(single, ghost_idx, source_idx)
            ghost_face = np.where(single, face_id, ghost_face)
        source_list.append(source_idx.astype(np.int32))
        ghost_list.append(ghost_face.astype(np.int32))
        bounce_list.append(bounce_idx.astype(np.int32))
    return np.concatenate(source_list), np.concatenate(ghost_list), np.concatenate(bounce_list)


def collide(pdfs, flags):
    speeds = jnp.asarray(VELOCITY_TABLE, jnp.float32)
    weights = jnp.asarray(WEIGHT_TABLE, jnp.float32)
    kernel = jnp.asarray(collision_matrix(), jnp.float32)
    density = jnp.sum(pdfs, axis=1)
    momentum = jnp.einsum("ia,bic->bac", speeds, pdfs, precision=lax.Precision.HIGHEST)
    projected = jnp.einsum("ia,bac->bic", speeds, momentum, precision=lax.Precision.HIGHEST)
    speed_sq = jnp.sum(momentum * momentum, axis=1)
    equilibrium = weights[None, :, None] * (density[:, None, :] + 3.0 * projected
                                            + (4.5 * projected * projected - 1.5 * speed_sq[:, None, :]) / REST_DENSITY)
    relaxed = pdfs - jnp.einsum("ij,bjc->bic", kernel, pdfs - equilibrium, precision=lax.Precision.HIGHEST)
    reflected = pdfs[:, opposite_table(), :]
    return jnp.where(flags[:, None, :] == 1, relaxed, reflected)


def outgoing_faces(post, edge):
    face_pops, face_cells = face_tables(edge)
    return post[:, face_pops[:, :, None], face_cells[:, None, :]]


def stream_blocks(post, ghost, missing, edge):
    source_idx, ghost_face, bounce_idx = stream_tables(edge)
    count = post.shape[0]
    combined = jnp.concatenate([post.reshape(count, -1), ghost.reshape(count, -1)], axis=1)
    read = jnp.take(combined, jnp.asarray(source_idx, jnp.int32), axis=1)
    bounced = jnp.take(post.reshape(count, -1), jnp.asarray(bounce_idx, jnp.int32), axis=1)
    lacking = jnp.zeros(read.shape, bool)
    for face_id in range(6):
        lacking = lacking | ((jnp.asarray(ghost_face, jnp.int32) == face_id)[None, :] & missing[:, face_id][:, None])
    return jnp.where(lacking, bounced, read).reshape(post.shape)


def reference(pdfs, plan, neighbours, flags):
    moved = jnp.zeros_like(pdfs).at[plan].set(pdfs)
    missing = neighbours < 0
    safe_ids = jnp.maximum(neighbours, 0)
    for step_id in range(STEPS):
        post = collide(moved, flags)
        faces = outgoing_faces(post, EDGE)
        ghost = faces[safe_ids, FACE_FLIP[None, :]]
        moved = stream_blocks(post, ghost, missing, EDGE)
    return moved
```

```python
import functools

import jax
import jax.numpy as jnp
import numpy as np
from jax import lax
from jax.experimental import pallas as pl
from jax.experimental.pallas import tpu as pltpu
from jax.sharding import PartitionSpec as P

EDGE = 16
BLK_DEV = 4
REACH = 2
STEPS = 3
POPS = 19
ROWS = EDGE**3 // 128
BLOCK_ROWS = POPS * ROWS
FACE_ROWS = 16
FACES = 6 * BLK_DEV
PEER_FACES = 6
OFFSETS = (-2, -1, 1, 2)
REST_DENSITY = 36.0
SHEAR_RATE = 1.6
VMEM_BYTES = 24 * 1024 * 1024

VELOCITIES = [
    (0, 0, 0), (1, 0, 0), (-1, 0, 0), (0, 1, 0), (0, -1, 0), (0, 0, 1), (0, 0, -1),
    (1, 1, 0), (-1, -1, 0), (1, -1, 0), (-1, 1, 0), (1, 0, 1), (-1, 0, -1), (1, 0, -1),
    (-1, 0, 1), (0, 1, 1), (0, -1, -1), (0, 1, -1), (0, -1, 1),
]
OPPOSITE = [VELOCITIES.index((-a, -b, -c)) for a, b, c in VELOCITIES]
FACE_POPS = [
    [i for i, c in enumerate(VELOCITIES) if c[face // 2] == (1 if face % 2 else -1)]
    for face in range(6)
]
WEIGHTS = [1.0 / 3.0] + [1.0 / 18.0] * 6 + [1.0 / 36.0] * 12


def moment_constants():
    c = np.array(VELOCITIES) * 1.0
    x, y, z = c[:, 0], c[:, 1], c[:, 2]
    s = x * x + y * y + z * z
    rows = {
        "e": 19 * s - 30,
        "eps": (21 * s * s - 53 * s + 24) / 2,
        "q": (5 * s - 9) * x,
        "pxx": 3 * x * x - s,
        "pixx": (3 * s - 5) * (3 * x * x - s),
        "pww": y * y - z * z,
        "piww": (3 * s - 5) * (y * y - z * z),
        "pxy": x * y,
        "m": x * (y * y - z * z),
    }
    rates = {
        "e": 1.19, "eps": 1.4, "q": 1.2, "pxx": SHEAR_RATE, "pixx": 1.4, "pww": SHEAR_RATE,
        "piww": 1.4, "pxy": SHEAR_RATE, "m": 1.98,
    }
    scale = {k: float(rates[k] / np.sum(rows[k] ** 2)) for k in rows}
    w = np.array(WEIGHTS)

    def of(row, term):
        return float(np.sum(rows[row] * w * term))

    square = [(4.5 * x * x - 1.5) / REST_DENSITY, (4.5 * y * y - 1.5) / REST_DENSITY,
              (4.5 * z * z - 1.5) / REST_DENSITY]
    terms = {
        "e_rho": of("e", 1.0), "eps_rho": of("eps", 1.0), "q_j": of("q", 3 * x),
        "pxy_jj": of("pxy", 9.0 * x * y / REST_DENSITY),
    }
    for name in ("e", "eps", "pxx", "pixx", "pww", "piww"):
        terms[name] = [of(name, t) for t in square]
    return scale, terms


SCALE, TERMS = moment_constants()


def relax(f):
    ex, ey, ez = f[1] + f[2], f[3] + f[4], f[5] + f[6]
    ox, oy, oz = f[1] - f[2], f[3] - f[4], f[5] - f[6]
    a, oa = f[7] + f[8], f[7] - f[8]
    b, ob = f[9] + f[10], f[9] - f[10]
    c, oc = f[11] + f[12], f[11] - f[12]
    d, od = f[13] + f[14], f[13] - f[14]
    g, og = f[15] + f[16], f[15] - f[16]
    h, oh = f[17] + f[18], f[17] - f[18]
    sxy, sxz, syz = a + b, c + d, g + h
    axial = ex + (ey + ez)
    diagonal = sxy + (sxz + syz)
    rho = f[0] + (axial + diagonal)
    xy_x, xz_x = oa + ob, oc + od
    xy_y, yz_y = oa - ob, og + oh
    xz_z, yz_z = oc - od, og - oh
    dx, dy, dz = xy_x + xz_x, xy_y + yz_y, xz_z + yz_z
    jx, jy, jz = ox + dx, oy + dy, oz + dz
    xx, yy, zz = jx * jx, jy * jy, jz * jz

    def even(name, value):
        k = TERMS[name]
        if abs(k[1] - k[2]) < 1e-12 and abs(k[0] - k[1]) < 1e-12:
            quad = (k[0] * SCALE[name]) * (xx + yy + zz)
        elif abs(k[0]) < 1e-12:
            quad = (k[1] * SCALE[name]) * (yy - zz)
        else:
            quad = (k[0] * SCALE[name]) * xx + (k[1] * SCALE[name]) * (yy + zz)
        return SCALE[name] * value - quad

    t_e = even("e", 8.0 * diagonal - 30.0 * f[0] - 11.0 * axial - TERMS["e_rho"] * rho)
    t_eps = even("eps", 12.0 * f[0] - 4.0 * axial + diagonal - TERMS["eps_rho"] * rho)
    p_axis = 2.0 * ex - (ey + ez)
    p_diag = (sxy + sxz) - 2.0 * syz
    w_axis = ey - ez
    w_diag = sxy - sxz
    t_pxx = even("pxx", p_axis + p_diag)
    t_pixx = even("pixx", p_diag - 2.0 * p_axis)
    t_pww = even("pww", w_axis + w_diag)
    t_piww = even("piww", w_diag - 2.0 * w_axis)
    k_p = TERMS["pxy_jj"]
    t_xy = SCALE["pxy"] * ((a - b) - k_p * (jx * jy))
    t_yz = SCALE["pxy"] * ((g - h) - k_p * (jy * jz))
    t_xz = SCALE["pxy"] * ((c - d) - k_p * (jx * jz))
    k_q = TERMS["q_j"]
    t_qx = SCALE["q"] * (dx - 4.0 * ox - k_q * jx)
    t_qy = SCALE["q"] * (dy - 4.0 * oy - k_q * jy)
    t_qz = SCALE["q"] * (dz - 4.0 * oz - k_q * jz)
    t_mx = SCALE["m"] * (xy_x - xz_x)
    t_my = SCALE["m"] * (yz_y - xy_y)
    t_mz = SCALE["m"] * (xz_z - yz_z)

    base_axis = -11.0 * t_e - 4.0 * t_eps
    base_diag = 8.0 * t_e + t_eps
    p1 = t_pxx - 2.0 * t_pixx
    w1 = t_pww - 2.0 * t_piww
    p2 = t_pxx + t_pixx
    w2 = t_pww + t_piww
    kx = base_axis + 2.0 * p1
    k_yz = base_axis - p1
    ky, kz = k_yz + w1, k_yz - w1
    near = base_diag + p2
    kxy, kxz, kyz = near + w2, near - w2, base_diag - 2.0 * p2
    qx4, qy4, qz4 = -4.0 * t_qx, -4.0 * t_qy, -4.0 * t_qz
    xp, xm = t_qx + t_mx, t_qx - t_mx
    yp, ym = t_qy + t_my, t_qy - t_my
    zp, zm = t_qz + t_mz, t_qz - t_mz
    pairs = [
        (kx, qx4), (ky, qy4), (kz, qz4),
        (kxy + t_xy, xp + ym), (kxy - t_xy, xp - ym),
        (kxz + t_xz, xm + zp), (kxz - t_xz, xm - zp),
        (kyz + t_yz, yp + zm), (kyz - t_yz, yp - zm),
    ]
    out = [f[0] - (12.0 * t_eps - 30.0 * t_e)]
    for n, (same, odd) in enumerate(pairs):
        out.append(f[2 * n + 1] - (same + odd))
        out.append(f[2 * n + 2] - (same - odd))
    return out


def collide_block(source, flags, target):
    for chunk in range(ROWS // 8):
        rows = [pl.ds(i * ROWS + chunk * 8, 8) for i in range(POPS)]
        f = [source(r) for r in rows]
        fluid = flags(pl.ds(chunk * 8, 8)) == 1
        post = relax(f)
        for i in range(POPS):
            target(rows[i], jnp.where(fluid, post[i], f[OPPOSITE[i]]))


def lanes_of(shape):
    return lax.broadcasted_iota(jnp.int32, shape, 1)


def roll_lanes(value, shift):
    shift %= 128
    return pltpu.roll(value, shift, 1) if shift else value


def pack_faces(load, store):
    lane = lanes_of((FACE_ROWS, 128))
    for face in (0, 1):
        first = 0 if face == 0 else ROWS - 2
        for k, i in enumerate(FACE_POPS[face]):
            store(face, slice(2 * k, 2 * k + 2), load(pl.ds(i * ROWS + first, 2)))
    for face in (2, 3):
        total = None
        for k, i in enumerate(FACE_POPS[face]):
            plane = load(pl.ds(i * ROWS + face - 2, EDGE, stride=2))
            plane = roll_lanes(plane, 16 * k if face == 2 else 16 * k - 112)
            total = plane if total is None else jnp.where(lane // 16 == k, plane, total)
        store(face, slice(0, FACE_ROWS), total)
    for face in (4, 5):
        total = None
        for half in range(2):
            for k, i in enumerate(FACE_POPS[face]):
                spot = 5 * half + k
                plane = load(pl.ds(i * ROWS + half * 16, 16))
                plane = roll_lanes(plane, spot if face == 4 else spot - 15)
                total = plane if total is None else jnp.where(lane % 16 == spot, plane, total)
        store(face, slice(0, FACE_ROWS), total)


def edge_mask(axis, part, row, lane):
    if axis == 0:
        return row < 2 if part > 0 else row >= ROWS - 2
    if axis == 1:
        if part > 0:
            return (row % 2 == 0) & (lane < 16)
        return (row % 2 == 1) & (lane >= 112)
    return lane % 16 == (0 if part > 0 else 15)


PAD = 8


def stream_block(load, ghost, wide, store):
    row = lax.broadcasted_iota(jnp.int32, (ROWS, 128), 0)
    lane = lanes_of((ROWS, 128))
    lane16 = lanes_of((16, 128))
    for i, (cx, cy, cz) in enumerate(VELOCITIES):
        shift = 16 * cy + cz
        faces = [0 if cx > 0 else 1, 2 if cy > 0 else 3, 4 if cz > 0 else 5]
        place = [FACE_POPS[face ^ 1].index(i) if part else None for face, part in zip(faces, (cx, cy, cz))]
        post = load(pl.ds(i * ROWS, ROWS))
        moved = roll_lanes(post, shift)
        if cz:
            plane = ghost(faces[2], slice(0, 16))
            spot = (0 if cz > 0 else 15) + 16 * cy
            incoming = jnp.concatenate(
                [roll_lanes(plane, spot - place[2]), roll_lanes(plane, spot - 5 - place[2])], axis=0
            )
            moved = jnp.where(lane % 16 == spot % 16, incoming, moved)
        if cx or cy:
            wide[i, PAD : PAD + ROWS, :] = moved
            if cx:
                two = ghost(faces[0], slice(2 * place[0], 2 * place[0] + 2))
                start = PAD - 2 if cx > 0 else PAD + ROWS
                wide[i, start : start + 2, :] = roll_lanes(two, shift)
            if cy:
                plane = ghost(faces[1], slice(0, 16))
                plane = roll_lanes(plane, (0 if cy > 0 else 112) - 16 * place[1] + cz)
                spots = pl.ds(PAD - 1 if cy > 0 else PAD + 2, EDGE, stride=2)
                keep = lane16 >= 16 if cy > 0 else lane16 < 112
                wide[i, spots, :] = jnp.where(keep, wide[i, spots, :], plane)
            moved = wide[i, PAD - 2 * cx : PAD - 2 * cx + ROWS, :]
            if cy:
                start = PAD - 2 * cx - cy
                across = wide[i, start : start + ROWS, :]
                moved = jnp.where(lane >= 16 if cy > 0 else lane < 112, moved, across)
        parts = [(axis, part) for axis, part in enumerate((cx, cy, cz)) if part]
        if len(parts) == 2:
            beyond = edge_mask(*parts[0], row, lane) & edge_mask(*parts[1], row, lane)
            moved = jnp.where(beyond, load(pl.ds(OPPOSITE[i] * ROWS, ROWS)), moved)
        store(pl.ds(i * ROWS, ROWS), moved)


def bounce_face(face, load, new_load, store):
    row = lax.broadcasted_iota(jnp.int32, (ROWS, 128), 0)
    lane = lanes_of((ROWS, 128))
    part = -1 if face % 2 else 1
    mask = edge_mask(face // 2, part, row, lane)
    for i in FACE_POPS[face ^ 1]:
        rows = pl.ds(i * ROWS, ROWS)
        store(rows, jnp.where(mask, load(pl.ds(OPPOSITE[i] * ROWS, ROWS)), new_load(rows)))


def cycle_offset(place, cycle):
    offset = lax.shift_right_arithmetic(place, 2) - lax.axis_index("blocks")
    offset = jnp.where(offset > REACH, offset - cycle, offset)
    return jnp.where(offset < -REACH, offset + cycle, offset)


def pack_kernel(cycle, plan, pdfs, *outs):
    offsets = [cycle_offset(plan[j], cycle) for j in range(BLK_DEV)]
    for out, offset in zip(outs, OFFSETS + (0,)):
        slot = jnp.int32(0)
        for j in range(BLK_DEV):
            slot = jnp.where(offsets[j] == offset, j, slot)
        for first in range(0, POPS, 8):
            count = min(8, POPS - first)
            for c in range(ROWS):
                out[pl.ds(first * ROWS + c, count, stride=ROWS), :] = pdfs[
                    slot, first : first + count, c * 128 : (c + 1) * 128
                ]


def index_kernel(cycle, neighbours, sends, receives, ranks):
    for n in range(FACES):
        sends[n] = 0
    for n in range((len(OFFSETS) + 1) * FACES):
        ranks[n] = -1
    counts = [jnp.int32(0) for _ in OFFSETS]
    for n in range(FACES):
        place = neighbours[n // 6, n % 6]
        offset = cycle_offset(place, cycle)
        across = (place & 3) * 6 + (n % 6 ^ 1)
        receives[n] = jnp.where(place < 0, -1, FACES + across)
        for o, value in enumerate(OFFSETS):
            mine = (place >= 0) & (offset == value)
            at = jnp.where(mine, o, len(OFFSETS)) * FACES
            ranks[at + across] = n

            @pl.when(mine & (counts[o] < PEER_FACES))
            def _(o=o, count=counts[o]):
                sends[o * PEER_FACES + count] = n

            counts[o] = counts[o] + mine.astype(jnp.int32)
    for o in range(len(OFFSETS)):
        seen = jnp.int32(0)
        for key in range(FACES):
            face = ranks[o * FACES + key]
            found = face >= 0

            @pl.when(found)
            def _(o=o, seen=seen, face=face):
                receives[face] = o * PEER_FACES + jnp.minimum(seen, PEER_FACES - 1)

            seen = seen + found.astype(jnp.int32)


def send_faces(sends, faces, outs):
    for o, out in enumerate(outs):
        for r in range(PEER_FACES):
            out[r * FACE_ROWS : (r + 1) * FACE_ROWS, :] = faces[sends[o * PEER_FACES + r]]


def pack_block(post, faces, b):
    def store(face, rows, value):
        faces[b * 6 + face, rows, :] = value

    pack_faces(lambda rows: post[b, rows, :], store)


def first_kernel(cycle, plan, sends, flags, *refs):
    arrived, (post, faces), outs = refs[:5], refs[5:7], refs[7:]
    for j in range(BLK_DEV):
        offset = cycle_offset(plan[j], cycle)
        slot = plan[j] & 3
        for source, value in zip(arrived, OFFSETS + (0,)):

            @pl.when(offset == value)
            def _(source=source):
                def store(rows, value):
                    post[slot, rows, :] = value

                collide_block(lambda r: source[r, :], lambda r: flags[slot, r, :], store)

    @pl.loop(0, BLK_DEV)
    def _(b):
        pack_block(post, faces, b)

    send_faces(sends, faces, outs)


def fill_pool(pool, arrived, own):
    for o, source in enumerate(arrived):
        for r in range(PEER_FACES):
            pool[o * PEER_FACES + r] = source[r * FACE_ROWS : (r + 1) * FACE_ROWS, :]
    pool[FACES:] = own[...]


def move_block(b, receives, post, pool, wide, new):
    spots = [receives[b * 6 + face] for face in range(6)]
    safe = [jnp.maximum(spot, 0) for spot in spots]

    def store(rows, value):
        new[rows, :] = value

    stream_block(
        lambda rows: post[b, rows, :],
        lambda face, rows: pool[safe[face], rows, :],
        wide,
        store,
    )
    for face in range(6):

        @pl.when(spots[face] < 0)
        def _(face=face):
            bounce_face(face, lambda rows: post[b, rows, :], lambda rows: new[rows, :], store)


def step_kernel(sends, receives, flags, post, own, *refs):
    arrived, (post_out, faces), outs, (pool, wide, new) = refs[:4], refs[4:6], refs[6:10], refs[10:]
    fill_pool(pool, arrived, own)

    @pl.loop(0, BLK_DEV)
    def _(b):
        move_block(b, receives, post, pool, wide, new)

        def store(rows, value):
            post_out[b, rows, :] = value

        collide_block(lambda r: new[r, :], lambda r: flags[b, r, :], store)
        pack_block(post_out, faces, b)

    send_faces(sends, faces, outs)


def last_kernel(receives, post, own, *refs):
    arrived, out, (pool, wide, new) = refs[:4], refs[4], refs[5:]
    fill_pool(pool, arrived, own)

    @pl.loop(0, BLK_DEV)
    def _(b):
        move_block(b, receives, post, pool, wide, new)
        for first in range(0, POPS, 8):
            count = min(8, POPS - first)
            for c in range(ROWS):
                out[b, first : first + count, c * 128 : (c + 1) * 128] = new[
                    pl.ds(first * ROWS + c, count, stride=ROWS), :
                ]


SMEM = pl.BlockSpec(memory_space=pltpu.SMEM)
VMEM = pl.BlockSpec(memory_space=pltpu.VMEM)
BLOCK = jax.ShapeDtypeStruct((BLOCK_ROWS, 128), jnp.float32)
POST = jax.ShapeDtypeStruct((BLK_DEV, BLOCK_ROWS, 128), jnp.float32)
OWN = jax.ShapeDtypeStruct((FACES, FACE_ROWS, 128), jnp.float32)
SENT = jax.ShapeDtypeStruct((PEER_FACES * FACE_ROWS, 128), jnp.float32)
MOVE_SCRATCH = [
    pltpu.VMEM((2 * FACES, FACE_ROWS, 128), jnp.float32),
    pltpu.VMEM((POPS, ROWS + 2 * PAD, 128), jnp.float32),
    pltpu.VMEM((BLOCK_ROWS, 128), jnp.float32),
]


def call(kernel, in_specs, out_shapes, out_specs, scratch=(), flops=0, bytes_accessed=0):
    return pl.pallas_call(
        kernel,
        in_specs=in_specs,
        out_shape=out_shapes,
        out_specs=out_specs,
        scratch_shapes=list(scratch),
        compiler_params=pltpu.CompilerParams(vmem_limit_bytes=VMEM_BYTES),
        cost_estimate=pl.CostEstimate(
            flops=flops, bytes_accessed=bytes_accessed, transcendentals=0
        ),
    )


def from_behind(value, distance, cycle):
    route = [((i - distance) % cycle, i) for i in range(cycle)]
    return lax.ppermute(value, "blocks", route)


def body(pdfs, plan, neighbours, flags):
    cycle = lax.axis_size("blocks")
    size = 4 * pdfs.size
    sent = call(
        functools.partial(pack_kernel, cycle), [SMEM, VMEM], [BLOCK] * 5, [VMEM] * 5,
        bytes_accessed=2 * size,
    )(plan, pdfs)
    arrived = [from_behind(value, o, cycle) for value, o in zip(sent, OFFSETS)] + [sent[4]]
    table = jax.ShapeDtypeStruct((FACES,), jnp.int32)
    sends, receives = call(
        functools.partial(index_kernel, cycle), [SMEM], [table] * 2, [SMEM] * 2,
        [pltpu.SMEM(((len(OFFSETS) + 1) * FACES,), jnp.int32)], bytes_accessed=1000,
    )(neighbours)
    cells = flags.reshape(BLK_DEV, ROWS, 128)
    post, own, *faces = call(
        functools.partial(first_kernel, cycle), [SMEM, SMEM, VMEM] + [VMEM] * 5,
        [POST, OWN] + [SENT] * 4, [VMEM] * 6, flops=300 * pdfs.size // POPS, bytes_accessed=2 * size,
    )(plan, sends, cells, *arrived)
    for _ in range(STEPS - 1):
        came = [from_behind(value, -o, cycle) for value, o in zip(faces[::-1], OFFSETS)]
        post, own, *faces = call(
            step_kernel, [SMEM, SMEM, VMEM, VMEM, VMEM] + [VMEM] * 4,
            [POST, OWN] + [SENT] * 4, [VMEM] * 6, MOVE_SCRATCH,
            flops=300 * pdfs.size // POPS, bytes_accessed=2 * size,
        )(sends, receives, cells, post, own, *came)
    came = [from_behind(value, -o, cycle) for value, o in zip(faces[::-1], OFFSETS)]
    return call(
        last_kernel, [SMEM, VMEM, VMEM] + [VMEM] * 4,
        jax.ShapeDtypeStruct(pdfs.shape, jnp.float32), VMEM, MOVE_SCRATCH,
        bytes_accessed=2 * size,
    )(receives, post, own, *came)


def solution(mesh):
    placed = (P("blocks", None, None), P("blocks"), P("blocks", None), P("blocks", None))
    return jax.shard_map(
        body, mesh=mesh, in_specs=placed, out_specs=P("blocks", None, None), check_vma=False
    )
```

```python
import functools

import jax
import jax.numpy as jnp
import numpy as np
from jax import lax
from jax.experimental import pallas as pl
from jax.experimental.pallas import tpu as pltpu
from jax.sharding import PartitionSpec as P

EDGE = 16
BLK_DEV = 4
REACH = 2
STEPS = 3
POPS = 19
ROWS = EDGE**3 // 128
BLOCK_ROWS = POPS * ROWS
FACE_ROWS = 16
FACES = 6 * BLK_DEV
PEER_FACES = 6
OFFSETS = (-2, -1, 1, 2)
REST_DENSITY = 36.0
SHEAR_RATE = 1.6
VMEM_BYTES = 24 * 1024 * 1024

VELOCITIES = [
    (0, 0, 0), (1, 0, 0), (-1, 0, 0), (0, 1, 0), (0, -1, 0), (0, 0, 1), (0, 0, -1),
    (1, 1, 0), (-1, -1, 0), (1, -1, 0), (-1, 1, 0), (1, 0, 1), (-1, 0, -1), (1, 0, -1),
    (-1, 0, 1), (0, 1, 1), (0, -1, -1), (0, 1, -1), (0, -1, 1),
]
OPPOSITE = [VELOCITIES.index((-a, -b, -c)) for a, b, c in VELOCITIES]
FACE_POPS = [
    [i for i, c in enumerate(VELOCITIES) if c[face // 2] == (1 if face % 2 else -1)]
    for face in range(6)
]
WEIGHTS = [1.0 / 3.0] + [1.0 / 18.0] * 6 + [1.0 / 36.0] * 12


def moment_constants():
    c = np.array(VELOCITIES) * 1.0
    x, y, z = c[:, 0], c[:, 1], c[:, 2]
    s = x * x + y * y + z * z
    rows = {
        "e": 19 * s - 30,
        "eps": (21 * s * s - 53 * s + 24) / 2,
        "q": (5 * s - 9) * x,
        "pxx": 3 * x * x - s,
        "pixx": (3 * s - 5) * (3 * x * x - s),
        "pww": y * y - z * z,
        "piww": (3 * s - 5) * (y * y - z * z),
        "pxy": x * y,
        "m": x * (y * y - z * z),
    }
    rates = {
        "e": 1.19, "eps": 1.4, "q": 1.2, "pxx": SHEAR_RATE, "pixx": 1.4, "pww": SHEAR_RATE,
        "piww": 1.4, "pxy": SHEAR_RATE, "m": 1.98,
    }
    scale = {k: float(rates[k] / np.sum(rows[k] ** 2)) for k in rows}
    w = np.array(WEIGHTS)

    def of(row, term):
        return float(np.sum(rows[row] * w * term))

    square = [(4.5 * x * x - 1.5) / REST_DENSITY, (4.5 * y * y - 1.5) / REST_DENSITY,
              (4.5 * z * z - 1.5) / REST_DENSITY]
    terms = {
        "e_rho": of("e", 1.0), "eps_rho": of("eps", 1.0), "q_j": of("q", 3 * x),
        "pxy_jj": of("pxy", 9.0 * x * y / REST_DENSITY),
    }
    for name in ("e", "eps", "pxx", "pixx", "pww", "piww"):
        terms[name] = [of(name, t) for t in square]
    return scale, terms


SCALE, TERMS = moment_constants()


def relax(f):
    ex, ey, ez = f[1] + f[2], f[3] + f[4], f[5] + f[6]
    ox, oy, oz = f[1] - f[2], f[3] - f[4], f[5] - f[6]
    a, oa = f[7] + f[8], f[7] - f[8]
    b, ob = f[9] + f[10], f[9] - f[10]
    c, oc = f[11] + f[12], f[11] - f[12]
    d, od = f[13] + f[14], f[13] - f[14]
    g, og = f[15] + f[16], f[15] - f[16]
    h, oh = f[17] + f[18], f[17] - f[18]
    sxy, sxz, syz = a + b, c + d, g + h
    axial = ex + (ey + ez)
    diagonal = sxy + (sxz + syz)
    rho = f[0] + (axial + diagonal)
    xy_x, xz_x = oa + ob, oc + od
    xy_y, yz_y = oa - ob, og + oh
    xz_z, yz_z = oc - od, og - oh
    dx, dy, dz = xy_x + xz_x, xy_y + yz_y, xz_z + yz_z
    jx, jy, jz = ox + dx, oy + dy, oz + dz
    xx, yy, zz = jx * jx, jy * jy, jz * jz

    def even(name, value):
        k = TERMS[name]
        if abs(k[1] - k[2]) < 1e-12 and abs(k[0] - k[1]) < 1e-12:
            quad = (k[0] * SCALE[name]) * (xx + yy + zz)
        elif abs(k[0]) < 1e-12:
            quad = (k[1] * SCALE[name]) * (yy - zz)
        else:
            quad = (k[0] * SCALE[name]) * xx + (k[1] * SCALE[name]) * (yy + zz)
        return SCALE[name] * value - quad

    t_e = even("e", 8.0 * diagonal - 30.0 * f[0] - 11.0 * axial - TERMS["e_rho"] * rho)
    t_eps = even("eps", 12.0 * f[0] - 4.0 * axial + diagonal - TERMS["eps_rho"] * rho)
    p_axis = 2.0 * ex - (ey + ez)
    p_diag = (sxy + sxz) - 2.0 * syz
    w_axis = ey - ez
    w_diag = sxy - sxz
    t_pxx = even("pxx", p_axis + p_diag)
    t_pixx = even("pixx", p_diag - 2.0 * p_axis)
    t_pww = even("pww", w_axis + w_diag)
    t_piww = even("piww", w_diag - 2.0 * w_axis)
    k_p = TERMS["pxy_jj"]
    t_xy = SCALE["pxy"] * ((a - b) - k_p * (jx * jy))
    t_yz = SCALE["pxy"] * ((g - h) - k_p * (jy * jz))
    t_xz = SCALE["pxy"] * ((c - d) - k_p * (jx * jz))
    k_q = TERMS["q_j"]
    t_qx = SCALE["q"] * (dx - 4.0 * ox - k_q * jx)
    t_qy = SCALE["q"] * (dy - 4.0 * oy - k_q * jy)
    t_qz = SCALE["q"] * (dz - 4.0 * oz - k_q * jz)
    t_mx = SCALE["m"] * (xy_x - xz_x)
    t_my = SCALE["m"] * (yz_y - xy_y)
    t_mz = SCALE["m"] * (xz_z - yz_z)

    base_axis = -11.0 * t_e - 4.0 * t_eps
    base_diag = 8.0 * t_e + t_eps
    p1 = t_pxx - 2.0 * t_pixx
    w1 = t_pww - 2.0 * t_piww
    p2 = t_pxx + t_pixx
    w2 = t_pww + t_piww
    kx = base_axis + 2.0 * p1
    k_yz = base_axis - p1
    ky, kz = k_yz + w1, k_yz - w1
    near = base_diag + p2
    kxy, kxz, kyz = near + w2, near - w2, base_diag - 2.0 * p2
    qx4, qy4, qz4 = -4.0 * t_qx, -4.0 * t_qy, -4.0 * t_qz
    xp, xm = t_qx + t_mx, t_qx - t_mx
    yp, ym = t_qy + t_my, t_qy - t_my
    zp, zm = t_qz + t_mz, t_qz - t_mz
    pairs = [
        (kx, qx4), (ky, qy4), (kz, qz4),
        (kxy + t_xy, xp + ym), (kxy - t_xy, xp - ym),
        (kxz + t_xz, xm + zp), (kxz - t_xz, xm - zp),
        (kyz + t_yz, yp + zm), (kyz - t_yz, yp - zm),
    ]
    out = [f[0] - (12.0 * t_eps - 30.0 * t_e)]
    for n, (same, odd) in enumerate(pairs):
        out.append(f[2 * n + 1] - (same + odd))
        out.append(f[2 * n + 2] - (same - odd))
    return out


def collide_block(source, flags, target):
    for chunk in range(ROWS // 8):
        rows = [pl.ds(i * ROWS + chunk * 8, 8) for i in range(POPS)]
        f = [source(r) for r in rows]
        fluid = flags(pl.ds(chunk * 8, 8)) == 1
        post = relax(f)
        for i in range(POPS):
            target(rows[i], jnp.where(fluid, post[i], f[OPPOSITE[i]]))


def lanes_of(shape):
    return lax.broadcasted_iota(jnp.int32, shape, 1)


def roll_lanes(value, shift):
    shift %= 128
    return pltpu.roll(value, shift, 1) if shift else value


def pack_faces(load, store):
    lane = lanes_of((FACE_ROWS, 128))
    for face in (0, 1):
        first = 0 if face == 0 else ROWS - 2
        for k, i in enumerate(FACE_POPS[face]):
            store(face, slice(2 * k, 2 * k + 2), load(pl.ds(i * ROWS + first, 2)))
    for face in (2, 3):
        total = None
        for k, i in enumerate(FACE_POPS[face]):
            plane = load(pl.ds(i * ROWS + face - 2, EDGE, stride=2))
            plane = roll_lanes(plane, 16 * k if face == 2 else 16 * k - 112)
            total = plane if total is None else jnp.where(lane // 16 == k, plane, total)
        store(face, slice(0, FACE_ROWS), total)
    for face in (4, 5):
        total = None
        for half in range(2):
            for k, i in enumerate(FACE_POPS[face]):
                spot = 5 * half + k
                plane = load(pl.ds(i * ROWS + half * 16, 16))
                plane = roll_lanes(plane, spot if face == 4 else spot - 15)
                total = plane if total is None else jnp.where(lane % 16 == spot, plane, total)
        store(face, slice(0, FACE_ROWS), total)


def edge_mask(axis, part, row, lane):
    if axis == 0:
        return row < 2 if part > 0 else row >= ROWS - 2
    if axis == 1:
        if part > 0:
            return (row % 2 == 0) & (lane < 16)
        return (row % 2 == 1) & (lane >= 112)
    return lane % 16 == (0 if part > 0 else 15)


PAD = 8


def stream_block(load, ghost, wide, store):
    row = lax.broadcasted_iota(jnp.int32, (ROWS, 128), 0)
    lane = lanes_of((ROWS, 128))
    lane16 = lanes_of((16, 128))
    for i, (cx, cy, cz) in enumerate(VELOCITIES):
        shift = 16 * cy + cz
        faces = [0 if cx > 0 else 1, 2 if cy > 0 else 3, 4 if cz > 0 else 5]
        place = [FACE_POPS[face ^ 1].index(i) if part else None for face, part in zip(faces, (cx, cy, cz))]
        post = load(pl.ds(i * ROWS, ROWS))
        moved = roll_lanes(post, shift)
        if cz:
            plane = ghost(faces[2], slice(0, 16))
            spot = (0 if cz > 0 else 15) + 16 * cy
            incoming = jnp.concatenate(
                [roll_lanes(plane, spot - place[2]), roll_lanes(plane, spot - 5 - place[2])], axis=0
            )
            moved = jnp.where(lane % 16 == spot % 16, incoming, moved)
        if cx or cy:
            wide[i, PAD : PAD + ROWS, :] = moved
            if cx:
                two = ghost(faces[0], slice(2 * place[0], 2 * place[0] + 2))
                start = PAD - 2 if cx > 0 else PAD + ROWS
                wide[i, start : start + 2, :] = roll_lanes(two, shift)
            if cy:
                plane = ghost(faces[1], slice(0, 16))
                plane = roll_lanes(plane, (0 if cy > 0 else 112) - 16 * place[1] + cz)
                spots = pl.ds(PAD - 1 if cy > 0 else PAD + 2, EDGE, stride=2)
                keep = lane16 >= 16 if cy > 0 else lane16 < 112
                wide[i, spots, :] = jnp.where(keep, wide[i, spots, :], plane)
            moved = wide[i, PAD - 2 * cx : PAD - 2 * cx + ROWS, :]
            if cy:
                start = PAD - 2 * cx - cy
                across = wide[i, start : start + ROWS, :]
                moved = jnp.where(lane >= 16 if cy > 0 else lane < 112, moved, across)
        parts = [(axis, part) for axis, part in enumerate((cx, cy, cz)) if part]
        if len(parts) == 2:
            beyond = edge_mask(*parts[0], row, lane) & edge_mask(*parts[1], row, lane)
            moved = jnp.where(beyond, load(pl.ds(OPPOSITE[i] * ROWS, ROWS)), moved)
        store(pl.ds(i * ROWS, ROWS), moved)


def bounce_face(face, load, new_load, store):
    row = lax.broadcasted_iota(jnp.int32, (ROWS, 128), 0)
    lane = lanes_of((ROWS, 128))
    part = -1 if face % 2 else 1
    mask = edge_mask(face // 2, part, row, lane)
    for i in FACE_POPS[face ^ 1]:
        rows = pl.ds(i * ROWS, ROWS)
        store(rows, jnp.where(mask, load(pl.ds(OPPOSITE[i] * ROWS, ROWS)), new_load(rows)))


def cycle_offset(place, cycle):
    offset = lax.shift_right_arithmetic(place, 2) - lax.axis_index("blocks")
    offset = jnp.where(offset > REACH, offset - cycle, offset)
    return jnp.where(offset < -REACH, offset + cycle, offset)


def pack_kernel(cycle, plan, pdfs, *outs):
    offsets = [cycle_offset(plan[j], cycle) for j in range(BLK_DEV)]
    values = [sent_offset(kind)[0] for kind in BLOCK_ORDER] + [0]
    for out, offset in zip(outs, values):
        slot = jnp.int32(0)
        for j in range(BLK_DEV):
            slot = jnp.where(offsets[j] == offset, j, slot)
        out[...] = pdfs[pl.ds(slot, BLOCK_ROWS, stride=BLK_DEV), :]


def index_kernel(cycle, neighbours, sends, receives, ranks):
    for n in range(FACES):
        sends[n] = 0
    for n in range((len(OFFSETS) + 1) * FACES):
        ranks[n] = -1
    counts = [jnp.int32(0) for _ in OFFSETS]
    for n in range(FACES):
        place = neighbours[n // 6, n % 6]
        offset = cycle_offset(place, cycle)
        across = (place & 3) * 6 + (n % 6 ^ 1)
        receives[n] = jnp.where(place < 0, -1, FACES + across)
        for o, value in enumerate(OFFSETS):
            mine = (place >= 0) & (offset == value)
            at = jnp.where(mine, o, len(OFFSETS)) * FACES
            ranks[at + across] = n

            @pl.when(mine & (counts[o] < PEER_FACES))
            def _(o=o, count=counts[o]):
                sends[o * PEER_FACES + count] = n

            counts[o] = counts[o] + mine.astype(jnp.int32)
    for o in range(len(OFFSETS)):
        seen = jnp.int32(0)
        for key in range(FACES):
            face = ranks[o * FACES + key]
            found = face >= 0

            @pl.when(found)
            def _(o=o, seen=seen, face=face):
                receives[face] = o * PEER_FACES + jnp.minimum(seen, PEER_FACES - 1)

            seen = seen + found.astype(jnp.int32)


ROUTES = {
    "p2": lambda i: i + 2,
    "m2": lambda i: i - 2,
    "p1": lambda i: i + 1,
    "m1": lambda i: i - 1,
    "x": lambda i: i + 1 if i % 2 else i - 1,
    "a": lambda i: i ^ 1,
}
BLOCK_ORDER = ('p2', 'x', 'm2', 'a')
FACE_ORDER = ('p2', 'x', 'm2', 'a')


def sent_offset(kind):
    core = lax.axis_index("blocks") & 1
    to = {"p2": 2, "m2": -2, "p1": 1, "m1": -1, "x": 2 * core - 1, "a": 1 - 2 * core}[kind]
    return to, -to if kind in ("x", "a") else to


def offset_place(offset):
    return offset + REACH - (offset > 0) if isinstance(offset, int) else (offset + 3) >> 1


def send_faces(sends, faces, outs):
    for kind, out in zip(FACE_ORDER, outs):
        o = offset_place(sent_offset(kind)[0])
        for r in range(PEER_FACES):
            out[r * FACE_ROWS : (r + 1) * FACE_ROWS, :] = faces[sends[o * PEER_FACES + r]]


def pack_block(post, faces, b):
    def store(face, rows, value):
        faces[b * 6 + face, rows, :] = value

    pack_faces(lambda rows: post[b, rows, :], store)


def flags_of(flags, b):
    return lambda rows: flags[pl.ds(BLK_DEV * rows.start + b, rows.size, stride=BLK_DEV), :]


def first_kernel(cycle, plan, sends, flags, *refs):
    arrived, (post, faces), outs = refs[:5], refs[5:7], refs[7:]
    values = [sent_offset(kind)[1] for kind in BLOCK_ORDER] + [0]
    for j in range(BLK_DEV):
        offset = cycle_offset(plan[j], cycle)
        slot = plan[j] & 3
        for source, value in zip(arrived, values):

            @pl.when(offset == value)
            def _(source=source):
                def store(rows, value):
                    post[slot, rows, :] = value

                collide_block(lambda r: source[r, :], flags_of(flags, slot), store)

    @pl.loop(0, BLK_DEV)
    def _(b):
        pack_block(post, faces, b)

    send_faces(sends, faces, outs)


def fill_pool(pool, arrived, own):
    for kind, source in zip(FACE_ORDER, arrived):
        o = offset_place(-sent_offset(kind)[1])
        for r in range(PEER_FACES):
            pool[o * PEER_FACES + r] = source[r * FACE_ROWS : (r + 1) * FACE_ROWS, :]
    pool[FACES:] = own[...]


def move_block(b, receives, post, pool, wide, new_load, store):
    spots = [receives[b * 6 + face] for face in range(6)]
    safe = [jnp.maximum(spot, 0) for spot in spots]
    stream_block(
        lambda rows: post[b, rows, :],
        lambda face, rows: pool[safe[face], rows, :],
        wide,
        store,
    )
    for face in range(6):

        @pl.when(spots[face] < 0)
        def _(face=face):
            bounce_face(face, lambda rows: post[b, rows, :], new_load, store)


def step_kernel(sends, receives, flags, post, own, *refs):
    arrived, (post_out, faces), outs, (pool, wide, new) = refs[:4], refs[4:6], refs[6:10], refs[10:]
    fill_pool(pool, arrived, own)

    @pl.loop(0, BLK_DEV)
    def _(b):
        def store_new(rows, value):
            new[rows, :] = value

        move_block(b, receives, post, pool, wide, lambda rows: new[rows, :], store_new)

        def store(rows, value):
            post_out[b, rows, :] = value

        collide_block(lambda r: new[r, :], flags_of(flags, b), store)
        pack_block(post_out, faces, b)

    send_faces(sends, faces, outs)


def last_kernel(receives, post, own, *refs):
    arrived, out, (pool, wide) = refs[:4], refs[4], refs[5:]
    fill_pool(pool, arrived, own)

    @pl.loop(0, BLK_DEV)
    def _(b):
        def spots(rows):
            return pl.ds(BLK_DEV * rows.start + b, rows.size, stride=BLK_DEV)

        def store(rows, value):
            out[spots(rows), :] = value

        move_block(b, receives, post, pool, wide, lambda rows: out[spots(rows), :], store)


SMEM = pl.BlockSpec(memory_space=pltpu.SMEM)
VMEM = pl.BlockSpec(memory_space=pltpu.VMEM)
BLOCK = jax.ShapeDtypeStruct((BLOCK_ROWS, 128), jnp.float32)
POST = jax.ShapeDtypeStruct((BLK_DEV, BLOCK_ROWS, 128), jnp.float32)
OWN = jax.ShapeDtypeStruct((FACES, FACE_ROWS, 128), jnp.float32)
SENT = jax.ShapeDtypeStruct((PEER_FACES * FACE_ROWS, 128), jnp.float32)
POOL = pltpu.VMEM((2 * FACES, FACE_ROWS, 128), jnp.float32)
WIDE = pltpu.VMEM((POPS, ROWS + 2 * PAD, 128), jnp.float32)
NEW = pltpu.VMEM((BLOCK_ROWS, 128), jnp.float32)


def call(kernel, in_specs, out_shapes, out_specs, scratch=(), flops=0, bytes_accessed=0):
    return pl.pallas_call(
        kernel,
        in_specs=in_specs,
        out_shape=out_shapes,
        out_specs=out_specs,
        scratch_shapes=list(scratch),
        compiler_params=pltpu.CompilerParams(vmem_limit_bytes=VMEM_BYTES),
        cost_estimate=pl.CostEstimate(
            flops=flops, bytes_accessed=bytes_accessed, transcendentals=0
        ),
    )


def exchange(buffers, order, cycle):
    return [
        lax.ppermute(value, "blocks", [(i, ROUTES[kind](i) % cycle) for i in range(cycle)])
        for value, kind in zip(buffers, order)
    ]


def body(pdfs, plan, neighbours, flags):
    cycle = lax.axis_size("blocks")
    size = 4 * pdfs.size
    rows = pdfs.transpose(1, 0, 2).reshape(POPS, BLK_DEV, ROWS, 128)
    rows = rows.transpose(0, 2, 1, 3).reshape(BLK_DEV * BLOCK_ROWS, 128)
    sent = call(
        functools.partial(pack_kernel, cycle), [SMEM, VMEM], [BLOCK] * 5, [VMEM] * 5,
        bytes_accessed=2 * size,
    )(plan, rows)
    arrived = exchange(sent, BLOCK_ORDER, cycle) + [sent[4]]
    table = jax.ShapeDtypeStruct((FACES,), jnp.int32)
    sends, receives = call(
        functools.partial(index_kernel, cycle), [SMEM], [table] * 2, [SMEM] * 2,
        [pltpu.SMEM(((len(OFFSETS) + 1) * FACES,), jnp.int32)], bytes_accessed=1000,
    )(neighbours)
    cells = flags.reshape(BLK_DEV, ROWS, 128).transpose(1, 0, 2).reshape(BLK_DEV * ROWS, 128)
    outs = dict(
        out_shapes=[POST, OWN] + [SENT] * 4, out_specs=[VMEM] * 6,
        flops=300 * pdfs.size // POPS, bytes_accessed=2 * size,
    )
    post, own, *faces = call(
        functools.partial(first_kernel, cycle), [SMEM, SMEM] + [VMEM] * 6, **outs
    )(plan, sends, cells, *arrived)
    for _ in range(STEPS - 1):
        came = exchange(faces, FACE_ORDER, cycle)
        post, own, *faces = call(
            step_kernel, [SMEM, SMEM] + [VMEM] * 7, scratch=[POOL, WIDE, NEW], **outs
        )(sends, receives, cells, post, own, *came)
    came = exchange(faces, FACE_ORDER, cycle)
    out = call(
        last_kernel, [SMEM] + [VMEM] * 6,
        jax.ShapeDtypeStruct((BLK_DEV * BLOCK_ROWS, 128), jnp.float32), VMEM, [POOL, WIDE],
        bytes_accessed=2 * size,
    )(receives, post, own, *came)
    out = out.reshape(POPS, ROWS, BLK_DEV, 128).transpose(2, 0, 1, 3)
    return out.reshape(pdfs.shape)


def solution(mesh):
    placed = (P("blocks", None, None), P("blocks"), P("blocks", None), P("blocks", None))
    return jax.shard_map(
        body, mesh=mesh, in_specs=placed, out_specs=P("blocks", None, None), check_vma=False
    )
```

```python
import functools

import jax
import jax.numpy as jnp
import numpy as np
from jax import lax
from jax.experimental import pallas as pl
from jax.experimental.pallas import tpu as pltpu
from jax.sharding import PartitionSpec as P

EDGE = 16
BLK_DEV = 4
REACH = 2
STEPS = 3
POPS = 19
ROWS = EDGE**3 // 128
BLOCK_ROWS = POPS * ROWS
FACE_ROWS = 16
FACES = 6 * BLK_DEV
PEER_FACES = 6
OFFSETS = (-2, -1, 1, 2)
REST_DENSITY = 36.0
SHEAR_RATE = 1.6
VMEM_BYTES = 24 * 1024 * 1024

VELOCITIES = [
    (0, 0, 0), (1, 0, 0), (-1, 0, 0), (0, 1, 0), (0, -1, 0), (0, 0, 1), (0, 0, -1),
    (1, 1, 0), (-1, -1, 0), (1, -1, 0), (-1, 1, 0), (1, 0, 1), (-1, 0, -1), (1, 0, -1),
    (-1, 0, 1), (0, 1, 1), (0, -1, -1), (0, 1, -1), (0, -1, 1),
]
OPPOSITE = [VELOCITIES.index((-a, -b, -c)) for a, b, c in VELOCITIES]
FACE_POPS = [
    [i for i, c in enumerate(VELOCITIES) if c[face // 2] == (1 if face % 2 else -1)]
    for face in range(6)
]
WEIGHTS = [1.0 / 3.0] + [1.0 / 18.0] * 6 + [1.0 / 36.0] * 12


def moment_constants():
    c = np.array(VELOCITIES) * 1.0
    x, y, z = c[:, 0], c[:, 1], c[:, 2]
    s = x * x + y * y + z * z
    rows = {
        "e": 19 * s - 30,
        "eps": (21 * s * s - 53 * s + 24) / 2,
        "q": (5 * s - 9) * x,
        "pxx": 3 * x * x - s,
        "pixx": (3 * s - 5) * (3 * x * x - s),
        "pww": y * y - z * z,
        "piww": (3 * s - 5) * (y * y - z * z),
        "pxy": x * y,
        "m": x * (y * y - z * z),
    }
    rates = {
        "e": 1.19, "eps": 1.4, "q": 1.2, "pxx": SHEAR_RATE, "pixx": 1.4, "pww": SHEAR_RATE,
        "piww": 1.4, "pxy": SHEAR_RATE, "m": 1.98,
    }
    scale = {k: float(rates[k] / np.sum(rows[k] ** 2)) for k in rows}
    w = np.array(WEIGHTS)

    def of(row, term):
        return float(np.sum(rows[row] * w * term))

    square = [(4.5 * x * x - 1.5) / REST_DENSITY, (4.5 * y * y - 1.5) / REST_DENSITY,
              (4.5 * z * z - 1.5) / REST_DENSITY]
    terms = {
        "e_rho": of("e", 1.0), "eps_rho": of("eps", 1.0), "q_j": of("q", 3 * x),
        "pxy_jj": of("pxy", 9.0 * x * y / REST_DENSITY),
    }
    for name in ("e", "eps", "pxx", "pixx", "pww", "piww"):
        terms[name] = [of(name, t) for t in square]
    return scale, terms


SCALE, TERMS = moment_constants()


def relax(f):
    ex, ey, ez = f[1] + f[2], f[3] + f[4], f[5] + f[6]
    ox, oy, oz = f[1] - f[2], f[3] - f[4], f[5] - f[6]
    a, oa = f[7] + f[8], f[7] - f[8]
    b, ob = f[9] + f[10], f[9] - f[10]
    c, oc = f[11] + f[12], f[11] - f[12]
    d, od = f[13] + f[14], f[13] - f[14]
    g, og = f[15] + f[16], f[15] - f[16]
    h, oh = f[17] + f[18], f[17] - f[18]
    sxy, sxz, syz = a + b, c + d, g + h
    axial = ex + (ey + ez)
    diagonal = sxy + (sxz + syz)
    rho = f[0] + (axial + diagonal)
    xy_x, xz_x = oa + ob, oc + od
    xy_y, yz_y = oa - ob, og + oh
    xz_z, yz_z = oc - od, og - oh
    dx, dy, dz = xy_x + xz_x, xy_y + yz_y, xz_z + yz_z
    jx, jy, jz = ox + dx, oy + dy, oz + dz
    xx, yy, zz = jx * jx, jy * jy, jz * jz

    def even(name, value):
        k = TERMS[name]
        if abs(k[1] - k[2]) < 1e-12 and abs(k[0] - k[1]) < 1e-12:
            quad = (k[0] * SCALE[name]) * (xx + yy + zz)
        elif abs(k[0]) < 1e-12:
            quad = (k[1] * SCALE[name]) * (yy - zz)
        else:
            quad = (k[0] * SCALE[name]) * xx + (k[1] * SCALE[name]) * (yy + zz)
        return SCALE[name] * value - quad

    t_e = even("e", 8.0 * diagonal - 30.0 * f[0] - 11.0 * axial - TERMS["e_rho"] * rho)
    t_eps = even("eps", 12.0 * f[0] - 4.0 * axial + diagonal - TERMS["eps_rho"] * rho)
    p_axis = 2.0 * ex - (ey + ez)
    p_diag = (sxy + sxz) - 2.0 * syz
    w_axis = ey - ez
    w_diag = sxy - sxz
    t_pxx = even("pxx", p_axis + p_diag)
    t_pixx = even("pixx", p_diag - 2.0 * p_axis)
    t_pww = even("pww", w_axis + w_diag)
    t_piww = even("piww", w_diag - 2.0 * w_axis)
    k_p = TERMS["pxy_jj"]
    t_xy = SCALE["pxy"] * ((a - b) - k_p * (jx * jy))
    t_yz = SCALE["pxy"] * ((g - h) - k_p * (jy * jz))
    t_xz = SCALE["pxy"] * ((c - d) - k_p * (jx * jz))
    k_q = TERMS["q_j"]
    t_qx = SCALE["q"] * (dx - 4.0 * ox - k_q * jx)
    t_qy = SCALE["q"] * (dy - 4.0 * oy - k_q * jy)
    t_qz = SCALE["q"] * (dz - 4.0 * oz - k_q * jz)
    t_mx = SCALE["m"] * (xy_x - xz_x)
    t_my = SCALE["m"] * (yz_y - xy_y)
    t_mz = SCALE["m"] * (xz_z - yz_z)

    base_axis = -11.0 * t_e - 4.0 * t_eps
    base_diag = 8.0 * t_e + t_eps
    p1 = t_pxx - 2.0 * t_pixx
    w1 = t_pww - 2.0 * t_piww
    p2 = t_pxx + t_pixx
    w2 = t_pww + t_piww
    kx = base_axis + 2.0 * p1
    k_yz = base_axis - p1
    ky, kz = k_yz + w1, k_yz - w1
    near = base_diag + p2
    kxy, kxz, kyz = near + w2, near - w2, base_diag - 2.0 * p2
    qx4, qy4, qz4 = -4.0 * t_qx, -4.0 * t_qy, -4.0 * t_qz
    xp, xm = t_qx + t_mx, t_qx - t_mx
    yp, ym = t_qy + t_my, t_qy - t_my
    zp, zm = t_qz + t_mz, t_qz - t_mz
    pairs = [
        (kx, qx4), (ky, qy4), (kz, qz4),
        (kxy + t_xy, xp + ym), (kxy - t_xy, xp - ym),
        (kxz + t_xz, xm + zp), (kxz - t_xz, xm - zp),
        (kyz + t_yz, yp + zm), (kyz - t_yz, yp - zm),
    ]
    out = [f[0] - (12.0 * t_eps - 30.0 * t_e)]
    for n, (same, odd) in enumerate(pairs):
        out.append(f[2 * n + 1] - (same + odd))
        out.append(f[2 * n + 2] - (same - odd))
    return out


def collide_block(source, flags, target):
    for chunk in range(ROWS // 8):
        rows = [pl.ds(i * ROWS + chunk * 8, 8) for i in range(POPS)]
        f = [source(r) for r in rows]
        fluid = flags(pl.ds(chunk * 8, 8)) == 1
        post = relax(f)
        for i in range(POPS):
            target(rows[i], jnp.where(fluid, post[i], f[OPPOSITE[i]]))


def lanes_of(shape):
    return lax.broadcasted_iota(jnp.int32, shape, 1)


def roll_lanes(value, shift):
    shift %= 128
    return pltpu.roll(value, shift, 1) if shift else value


def pack_faces(load, store):
    lane = lanes_of((FACE_ROWS, 128))
    for face in (0, 1):
        first = 0 if face == 0 else ROWS - 2
        for k, i in enumerate(FACE_POPS[face]):
            store(face, slice(2 * k, 2 * k + 2), load(pl.ds(i * ROWS + first, 2)))
    for face in (2, 3):
        total = None
        for k, i in enumerate(FACE_POPS[face]):
            plane = load(pl.ds(i * ROWS + face - 2, EDGE, stride=2))
            plane = roll_lanes(plane, 16 * k if face == 2 else 16 * k - 112)
            total = plane if total is None else jnp.where(lane // 16 == k, plane, total)
        store(face, slice(0, FACE_ROWS), total)
    for face in (4, 5):
        total = None
        for half in range(2):
            for k, i in enumerate(FACE_POPS[face]):
                spot = 5 * half + k
                plane = load(pl.ds(i * ROWS + half * 16, 16))
                plane = roll_lanes(plane, spot if face == 4 else spot - 15)
                total = plane if total is None else jnp.where(lane % 16 == spot, plane, total)
        store(face, slice(0, FACE_ROWS), total)


def edge_mask(axis, part, row, lane):
    if axis == 0:
        return row < 2 if part > 0 else row >= ROWS - 2
    if axis == 1:
        if part > 0:
            return (row % 2 == 0) & (lane < 16)
        return (row % 2 == 1) & (lane >= 112)
    return lane % 16 == (0 if part > 0 else 15)


PAD = 8


def double_mask(parts, row, lane):
    return edge_mask(*parts[0], row, lane) & edge_mask(*parts[1], row, lane)


def stream_inside(load, wide, store):
    row = lax.broadcasted_iota(jnp.int32, (ROWS, 128), 0)
    lane = lanes_of((ROWS, 128))
    for i, (cx, cy, cz) in enumerate(VELOCITIES):
        moved = roll_lanes(load(pl.ds(i * ROWS, ROWS)), 16 * cy + cz)
        if cx or cy:
            wide[i, PAD : PAD + ROWS, :] = moved
            moved = wide[i, PAD - 2 * cx : PAD - 2 * cx + ROWS, :]
            if cy:
                start = PAD - 2 * cx - cy
                across = wide[i, start : start + ROWS, :]
                moved = jnp.where(lane >= 16 if cy > 0 else lane < 112, moved, across)
        parts = [(axis, part) for axis, part in enumerate((cx, cy, cz)) if part]
        if len(parts) == 2:
            beyond = double_mask(parts, row, lane)
            moved = jnp.where(beyond, load(pl.ds(OPPOSITE[i] * ROWS, ROWS)), moved)
        store(pl.ds(i * ROWS, ROWS), moved)


def fill_ghosts(pops, base, ghost, target):
    row = lax.broadcasted_iota(jnp.int32, (ROWS, 128), 0)
    lane = lanes_of((ROWS, 128))
    row2 = lax.broadcasted_iota(jnp.int32, (2, 128), 0)
    lane2 = lanes_of((2, 128))
    row16 = lax.broadcasted_iota(jnp.int32, (16, 128), 0)
    lane16 = lanes_of((16, 128))
    for i in pops:
        cx, cy, cz = VELOCITIES[i]
        faces = [0 if cx > 0 else 1, 2 if cy > 0 else 3, 4 if cz > 0 else 5]
        place = [FACE_POPS[face ^ 1].index(i) if part else None for face, part in zip(faces, (cx, cy, cz))]
        value = base(pl.ds(i * ROWS, ROWS))
        if cz:
            plane = ghost(faces[2], slice(0, 16))
            spot = (0 if cz > 0 else 15) + 16 * cy
            incoming = jnp.concatenate(
                [roll_lanes(plane, spot - place[2]), roll_lanes(plane, spot - 5 - place[2])], axis=0
            )
            if cx:
                incoming = pltpu.roll(incoming, 2 * cx % ROWS, 0)
            if cy:
                across = pltpu.roll(incoming, cy % ROWS, 0)
                incoming = jnp.where(lane >= 16 if cy > 0 else lane < 112, incoming, across)
            mask = edge_mask(2, cz, row, lane)
            for axis, part in ((0, cx), (1, cy)):
                if part:
                    mask = mask & jnp.logical_not(edge_mask(axis, part, row, lane))
            value = jnp.where(mask, incoming, value)
        target[pl.ds(i * ROWS, ROWS), :] = value
        if cx:
            two = roll_lanes(ghost(faces[0], slice(2 * place[0], 2 * place[0] + 2)), 16 * cy + cz)
            spots = pl.ds(i * ROWS + (0 if cx > 0 else ROWS - 2), 2)
            if cy:
                swapped = jnp.concatenate([two[1:2], two[0:1]], axis=0)
                two = jnp.where(lane2 >= 16 if cy > 0 else lane2 < 112, two, swapped)
                two = jnp.where(edge_mask(1, cy, row2, lane2), target[spots, :], two)
            if cz:
                two = jnp.where(edge_mask(2, cz, row2, lane2), target[spots, :], two)
            target[spots, :] = two
        if cy:
            plane = roll_lanes(
                ghost(faces[1], slice(0, 16)), (0 if cy > 0 else 112) - 16 * place[1] + cz
            )
            mask = lane16 < 16 if cy > 0 else lane16 >= 112
            if cx:
                plane = pltpu.roll(plane, cx % EDGE, 0)
                mask = mask & (row16 != (0 if cx > 0 else EDGE - 1))
            if cz:
                mask = mask & jnp.logical_not(edge_mask(2, cz, row16, lane16))
            spots = pl.ds(i * ROWS + (0 if cy > 0 else 1), EDGE, stride=2)
            target[spots, :] = jnp.where(mask, plane, target[spots, :])


def bounce_face(face, load, new_load, store):
    row = lax.broadcasted_iota(jnp.int32, (ROWS, 128), 0)
    lane = lanes_of((ROWS, 128))
    part = -1 if face % 2 else 1
    mask = edge_mask(face // 2, part, row, lane)
    for i in FACE_POPS[face ^ 1]:
        rows = pl.ds(i * ROWS, ROWS)
        store(rows, jnp.where(mask, load(pl.ds(OPPOSITE[i] * ROWS, ROWS)), new_load(rows)))


def cycle_offset(place, cycle):
    offset = lax.shift_right_arithmetic(place, 2) - lax.axis_index("blocks")
    offset = jnp.where(offset > REACH, offset - cycle, offset)
    return jnp.where(offset < -REACH, offset + cycle, offset)


def pack_kernel(moves, pdfs, *outs):
    values = [sent_offset(kind)[0] for kind in BLOCK_ORDER] + [0]
    for out, value in zip(outs, values):
        source = jnp.int32(0)
        for j in range(BLK_DEV):
            source = jnp.where(moves[j] == value, j, source)
        out[...] = pdfs[pl.ds(source, BLOCK_ROWS, stride=BLK_DEV), :]


def index_kernel(cycle, neighbours, sends, receives, ranks):
    for n in range(FACES):
        sends[n] = 0
    for n in range((len(OFFSETS) + 1) * FACES):
        ranks[n] = -1
    counts = [jnp.int32(0) for _ in OFFSETS]
    for n in range(FACES):
        place = neighbours[n // 6, n % 6]
        offset = cycle_offset(place, cycle)
        across = (place & 3) * 6 + (n % 6 ^ 1)
        receives[n] = jnp.where(place < 0, -1, FACES + across)
        for o, value in enumerate(OFFSETS):
            mine = (place >= 0) & (offset == value)
            at = jnp.where(mine, o, len(OFFSETS)) * FACES
            ranks[at + across] = n

            @pl.when(mine & (counts[o] < PEER_FACES))
            def _(o=o, count=counts[o]):
                sends[o * PEER_FACES + count] = n

            counts[o] = counts[o] + mine.astype(jnp.int32)
    for o in range(len(OFFSETS)):
        seen = jnp.int32(0)
        for key in range(FACES):
            face = ranks[o * FACES + key]
            found = face >= 0

            @pl.when(found)
            def _(o=o, seen=seen, face=face):
                receives[face] = o * PEER_FACES + jnp.minimum(seen, PEER_FACES - 1)

            seen = seen + found.astype(jnp.int32)


ROUTES = {
    "p2": lambda i: i + 2,
    "m2": lambda i: i - 2,
    "p1": lambda i: i + 1,
    "m1": lambda i: i - 1,
    "x": lambda i: i + 1 if i % 2 else i - 1,
    "a": lambda i: i ^ 1,
}
BLOCK_ORDER = ('p2', 'x', 'm2', 'a')
FACE_ORDER = ('p2', 'x', 'm2', 'a')


def sent_offset(kind):
    core = lax.axis_index("blocks") & 1
    to = {"p2": 2, "m2": -2, "p1": 1, "m1": -1, "x": 2 * core - 1, "a": 1 - 2 * core}[kind]
    return to, -to if kind in ("x", "a") else to


def offset_place(offset):
    return offset + REACH - (offset > 0) if isinstance(offset, int) else (offset + 3) >> 1


def send_faces(sends, faces, outs):
    for kind, out in zip(FACE_ORDER, outs):
        o = offset_place(sent_offset(kind)[0])
        for r in range(PEER_FACES):
            out[r * FACE_ROWS : (r + 1) * FACE_ROWS, :] = faces[sends[o * PEER_FACES + r]]


def pack_block(post, faces, b):
    def store(face, rows, value):
        faces[b * 6 + face, rows, :] = value

    pack_faces(lambda rows: post[b, rows, :], store)


def flags_of(flags, b):
    return lambda rows: flags[pl.ds(BLK_DEV * rows.start + b, rows.size, stride=BLK_DEV), :]


def first_kernel(moves, sends, flags, *refs):
    arrived, (post, faces), outs = refs[:5], refs[5:7], refs[7:]
    values = [sent_offset(kind)[1] for kind in BLOCK_ORDER] + [0]
    for j in range(BLK_DEV):
        slot = moves[BLK_DEV + j]
        for source, value in zip(arrived, values):

            @pl.when(moves[j] == value)
            def _(source=source):
                def store(rows, value):
                    post[slot, rows, :] = value

                collide_block(lambda r: source[r, :], flags_of(flags, slot), store)

    @pl.loop(0, BLK_DEV)
    def _(b):
        pack_block(post, faces, b)

    send_faces(sends, faces, outs)


def fill_pool(pool, arrived, own):
    for kind, source in zip(FACE_ORDER, arrived):
        o = offset_place(-sent_offset(kind)[1])
        for r in range(PEER_FACES):
            pool[o * PEER_FACES + r] = source[r * FACE_ROWS : (r + 1) * FACE_ROWS, :]
    pool[FACES:] = own[...]


def inside_kernel(post, new, wide):
    @pl.loop(0, BLK_DEV)
    def _(b):
        def store(rows, value):
            new[b, rows, :] = value

        stream_inside(lambda rows: post[b, rows, :], wide, store)


def fill_block(b, pops, receives, inside, pool, new):
    spots = [jnp.maximum(receives[b * 6 + face], 0) for face in range(6)]
    fill_ghosts(
        pops,
        lambda rows: inside[b, rows, :],
        lambda face, rows: pool[spots[face], rows, :],
        new,
    )


def bounce_block(b, receives, post, new):
    def store(rows, value):
        new[rows, :] = value

    for face in range(6):

        @pl.when(receives[b * 6 + face] < 0)
        def _(face=face):
            bounce_face(face, lambda rows: post[b, rows, :], lambda rows: new[rows, :], store)


def step_kernel(sends, receives, flags, post, inside, own, *refs):
    arrived, (post_out, faces), outs, (pool, new) = refs[:4], refs[4:6], refs[6:10], refs[10:]
    fill_pool(pool, arrived, own)

    @pl.loop(0, BLK_DEV)
    def _(b):
        fill_block(b, range(POPS), receives, inside, pool, new)
        bounce_block(b, receives, post, new)

        def store(rows, value):
            post_out[b, rows, :] = value

        collide_block(lambda r: new[r, :], flags_of(flags, b), store)
        pack_block(post_out, faces, b)

    send_faces(sends, faces, outs)


def last_kernel(receives, post, inside, own, *refs):
    arrived, out, (pool, new, whole, sem) = refs[:4], refs[4], refs[5:]
    fill_pool(pool, arrived, own)

    def store_out(i):
        for b in range(BLK_DEV):
            whole[pl.ds(i * ROWS * BLK_DEV + b, ROWS, stride=BLK_DEV), :] = new[
                b, i * ROWS : (i + 1) * ROWS, :
            ]
        rows = pl.ds(i * ROWS * BLK_DEV, ROWS * BLK_DEV)
        copy = pltpu.make_async_copy(whole.at[rows, :], out.at[rows, :], sem.at[i])
        copy.start()
        return copy

    copies = []
    for i in range(POPS):
        for b in range(BLK_DEV):
            fill_block(b, [i], receives, inside, pool, new.at[b])
        copies.append(store_out(i))
    for copy in copies:
        copy.wait()
    least = receives[0]
    for n in range(1, FACES):
        least = jnp.minimum(least, receives[n])

    @pl.when(least < 0)
    def _():
        for b in range(BLK_DEV):
            bounce_block(b, receives, post, new.at[b])
        for copy in [store_out(i) for i in range(POPS)]:
            copy.wait()


SMEM = pl.BlockSpec(memory_space=pltpu.SMEM)
VMEM = pl.BlockSpec(memory_space=pltpu.VMEM)
HBM = pl.BlockSpec(memory_space=pltpu.HBM)
BLOCK = jax.ShapeDtypeStruct((BLOCK_ROWS, 128), jnp.float32)
POST = jax.ShapeDtypeStruct((BLK_DEV, BLOCK_ROWS, 128), jnp.float32)
OWN = jax.ShapeDtypeStruct((FACES, FACE_ROWS, 128), jnp.float32)
SENT = jax.ShapeDtypeStruct((PEER_FACES * FACE_ROWS, 128), jnp.float32)
POOL = pltpu.VMEM((2 * FACES, FACE_ROWS, 128), jnp.float32)
WIDE = pltpu.VMEM((POPS, ROWS + 2 * PAD, 128), jnp.float32)
NEW = pltpu.VMEM((BLOCK_ROWS, 128), jnp.float32)


def call(
    kernel, in_specs, out_shapes, out_specs, scratch=(), flops=0, bytes_accessed=0
):
    return pl.pallas_call(
        kernel,
        in_specs=in_specs,
        out_shape=out_shapes,
        out_specs=out_specs,
        scratch_shapes=list(scratch),
        compiler_params=pltpu.CompilerParams(vmem_limit_bytes=VMEM_BYTES),
        cost_estimate=pl.CostEstimate(
            flops=flops, bytes_accessed=bytes_accessed, transcendentals=0
        ),
    )


def exchange(buffers, order, cycle):
    return [
        lax.ppermute(value, "blocks", [(i, ROUTES[kind](i) % cycle) for i in range(cycle)])
        for value, kind in zip(buffers, order)
    ]


def body(pdfs, plan, neighbours, flags):
    cycle = lax.axis_size("blocks")
    size = 4 * pdfs.size
    rows = pdfs.transpose(1, 0, 2).reshape(POPS, BLK_DEV, ROWS, 128)
    rows = rows.transpose(0, 2, 1, 3).reshape(BLK_DEV * BLOCK_ROWS, 128)
    moves = jnp.concatenate([cycle_offset(plan, cycle), plan & 3])
    sent = call(
        pack_kernel, [SMEM, VMEM], [BLOCK] * 5, [VMEM] * 5, bytes_accessed=2 * size
    )(moves, rows)
    arrived = exchange(sent, BLOCK_ORDER, cycle) + [sent[4]]
    table = jax.ShapeDtypeStruct((FACES,), jnp.int32)
    sends, receives = call(
        functools.partial(index_kernel, cycle), [SMEM], [table] * 2, [SMEM] * 2,
        [pltpu.SMEM(((len(OFFSETS) + 1) * FACES,), jnp.int32)], bytes_accessed=1000,
    )(neighbours)
    cells = flags.reshape(BLK_DEV, ROWS, 128).transpose(1, 0, 2).reshape(BLK_DEV * ROWS, 128)
    outs = dict(
        out_shapes=[POST, OWN] + [SENT] * 4, out_specs=[VMEM] * 6,
        flops=300 * pdfs.size // POPS, bytes_accessed=2 * size,
    )
    inside = call(inside_kernel, [VMEM], POST, VMEM, [WIDE], bytes_accessed=2 * size)
    post, own, *faces = call(
        first_kernel, [SMEM, SMEM] + [VMEM] * 6, **outs
    )(moves, sends, cells, *arrived)
    for _ in range(STEPS - 1):
        came = exchange(faces, FACE_ORDER, cycle)
        post, own, *faces = call(
            step_kernel, [SMEM, SMEM] + [VMEM] * 8, scratch=[POOL, NEW], **outs
        )(sends, receives, cells, post, inside(post), own, *came)
    came = exchange(faces, FACE_ORDER, cycle)
    whole = (BLK_DEV * BLOCK_ROWS, 128)
    out = call(
        last_kernel, [SMEM] + [VMEM] * 7,
        jax.ShapeDtypeStruct(whole, jnp.float32), HBM,
        [POOL, pltpu.VMEM(POST.shape, jnp.float32), pltpu.VMEM(whole, jnp.float32),
         pltpu.SemaphoreType.DMA((POPS,))],
        bytes_accessed=2 * size,
    )(receives, post, inside(post), own, *came)
    out = out.reshape(POPS, ROWS, BLK_DEV, 128).transpose(2, 0, 1, 3)
    return out.reshape(pdfs.shape)


def solution(mesh):
    placed = (P("blocks", None, None), P("blocks"), P("blocks", None), P("blocks", None))
    return jax.shard_map(
        body, mesh=mesh, in_specs=placed, out_specs=P("blocks", None, None), check_vma=False
    )
```

```python
import functools

import jax
import jax.numpy as jnp
import numpy as np
from jax import lax
from jax.experimental import pallas as pl
from jax.experimental.pallas import tpu as pltpu
from jax.sharding import PartitionSpec as P

EDGE = 16
BLK_DEV = 4
REACH = 2
STEPS = 3
POPS = 19
ROWS = EDGE**3 // 128
BLOCK_ROWS = POPS * ROWS
FACE_ROWS = 16
FACES = 6 * BLK_DEV
PEER_FACES = 6
OFFSETS = (-2, -1, 1, 2)
REST_DENSITY = 36.0
SHEAR_RATE = 1.6
VMEM_BYTES = 24 * 1024 * 1024

VELOCITIES = [
    (0, 0, 0), (1, 0, 0), (-1, 0, 0), (0, 1, 0), (0, -1, 0), (0, 0, 1), (0, 0, -1),
    (1, 1, 0), (-1, -1, 0), (1, -1, 0), (-1, 1, 0), (1, 0, 1), (-1, 0, -1), (1, 0, -1),
    (-1, 0, 1), (0, 1, 1), (0, -1, -1), (0, 1, -1), (0, -1, 1),
]
OPPOSITE = [VELOCITIES.index((-a, -b, -c)) for a, b, c in VELOCITIES]
FACE_POPS = [
    [i for i, c in enumerate(VELOCITIES) if c[face // 2] == (1 if face % 2 else -1)]
    for face in range(6)
]
WEIGHTS = [1.0 / 3.0] + [1.0 / 18.0] * 6 + [1.0 / 36.0] * 12


def moment_constants():
    c = np.array(VELOCITIES) * 1.0
    x, y, z = c[:, 0], c[:, 1], c[:, 2]
    s = x * x + y * y + z * z
    rows = {
        "e": 19 * s - 30,
        "eps": (21 * s * s - 53 * s + 24) / 2,
        "q": (5 * s - 9) * x,
        "pxx": 3 * x * x - s,
        "pixx": (3 * s - 5) * (3 * x * x - s),
        "pww": y * y - z * z,
        "piww": (3 * s - 5) * (y * y - z * z),
        "pxy": x * y,
        "m": x * (y * y - z * z),
    }
    rates = {
        "e": 1.19, "eps": 1.4, "q": 1.2, "pxx": SHEAR_RATE, "pixx": 1.4, "pww": SHEAR_RATE,
        "piww": 1.4, "pxy": SHEAR_RATE, "m": 1.98,
    }
    scale = {k: float(rates[k] / np.sum(rows[k] ** 2)) for k in rows}
    w = np.array(WEIGHTS)

    def of(row, term):
        return float(np.sum(rows[row] * w * term))

    square = [(4.5 * x * x - 1.5) / REST_DENSITY, (4.5 * y * y - 1.5) / REST_DENSITY,
              (4.5 * z * z - 1.5) / REST_DENSITY]
    terms = {
        "e_rho": of("e", 1.0), "eps_rho": of("eps", 1.0), "q_j": of("q", 3 * x),
        "pxy_jj": of("pxy", 9.0 * x * y / REST_DENSITY),
    }
    for name in ("e", "eps", "pxx", "pixx", "pww", "piww"):
        terms[name] = [of(name, t) for t in square]
    return scale, terms


SCALE, TERMS = moment_constants()


def relax(f):
    ex, ey, ez = f[1] + f[2], f[3] + f[4], f[5] + f[6]
    ox, oy, oz = f[1] - f[2], f[3] - f[4], f[5] - f[6]
    a, oa = f[7] + f[8], f[7] - f[8]
    b, ob = f[9] + f[10], f[9] - f[10]
    c, oc = f[11] + f[12], f[11] - f[12]
    d, od = f[13] + f[14], f[13] - f[14]
    g, og = f[15] + f[16], f[15] - f[16]
    h, oh = f[17] + f[18], f[17] - f[18]
    sxy, sxz, syz = a + b, c + d, g + h
    axial = ex + (ey + ez)
    diagonal = sxy + (sxz + syz)
    rho = f[0] + (axial + diagonal)
    xy_x, xz_x = oa + ob, oc + od
    xy_y, yz_y = oa - ob, og + oh
    xz_z, yz_z = oc - od, og - oh
    dx, dy, dz = xy_x + xz_x, xy_y + yz_y, xz_z + yz_z
    jx, jy, jz = ox + dx, oy + dy, oz + dz
    xx, yy, zz = jx * jx, jy * jy, jz * jz

    def even(name, value):
        k = TERMS[name]
        if abs(k[1] - k[2]) < 1e-12 and abs(k[0] - k[1]) < 1e-12:
            quad = (k[0] * SCALE[name]) * (xx + yy + zz)
        elif abs(k[0]) < 1e-12:
            quad = (k[1] * SCALE[name]) * (yy - zz)
        else:
            quad = (k[0] * SCALE[name]) * xx + (k[1] * SCALE[name]) * (yy + zz)
        return SCALE[name] * value - quad

    t_e = even("e", 8.0 * diagonal - 30.0 * f[0] - 11.0 * axial - TERMS["e_rho"] * rho)
    t_eps = even("eps", 12.0 * f[0] - 4.0 * axial + diagonal - TERMS["eps_rho"] * rho)
    p_axis = 2.0 * ex - (ey + ez)
    p_diag = (sxy + sxz) - 2.0 * syz
    w_axis = ey - ez
    w_diag = sxy - sxz
    t_pxx = even("pxx", p_axis + p_diag)
    t_pixx = even("pixx", p_diag - 2.0 * p_axis)
    t_pww = even("pww", w_axis + w_diag)
    t_piww = even("piww", w_diag - 2.0 * w_axis)
    k_p = TERMS["pxy_jj"]
    t_xy = SCALE["pxy"] * ((a - b) - k_p * (jx * jy))
    t_yz = SCALE["pxy"] * ((g - h) - k_p * (jy * jz))
    t_xz = SCALE["pxy"] * ((c - d) - k_p * (jx * jz))
    k_q = TERMS["q_j"]
    t_qx = SCALE["q"] * (dx - 4.0 * ox - k_q * jx)
    t_qy = SCALE["q"] * (dy - 4.0 * oy - k_q * jy)
    t_qz = SCALE["q"] * (dz - 4.0 * oz - k_q * jz)
    t_mx = SCALE["m"] * (xy_x - xz_x)
    t_my = SCALE["m"] * (yz_y - xy_y)
    t_mz = SCALE["m"] * (xz_z - yz_z)

    base_axis = -11.0 * t_e - 4.0 * t_eps
    base_diag = 8.0 * t_e + t_eps
    p1 = t_pxx - 2.0 * t_pixx
    w1 = t_pww - 2.0 * t_piww
    p2 = t_pxx + t_pixx
    w2 = t_pww + t_piww
    kx = base_axis + 2.0 * p1
    k_yz = base_axis - p1
    ky, kz = k_yz + w1, k_yz - w1
    near = base_diag + p2
    kxy, kxz, kyz = near + w2, near - w2, base_diag - 2.0 * p2
    qx4, qy4, qz4 = -4.0 * t_qx, -4.0 * t_qy, -4.0 * t_qz
    xp, xm = t_qx + t_mx, t_qx - t_mx
    yp, ym = t_qy + t_my, t_qy - t_my
    zp, zm = t_qz + t_mz, t_qz - t_mz
    pairs = [
        (kx, qx4), (ky, qy4), (kz, qz4),
        (kxy + t_xy, xp + ym), (kxy - t_xy, xp - ym),
        (kxz + t_xz, xm + zp), (kxz - t_xz, xm - zp),
        (kyz + t_yz, yp + zm), (kyz - t_yz, yp - zm),
    ]
    out = [f[0] - (12.0 * t_eps - 30.0 * t_e)]
    for n, (same, odd) in enumerate(pairs):
        out.append(f[2 * n + 1] - (same + odd))
        out.append(f[2 * n + 2] - (same - odd))
    return out


def collide_block(source, flags, target):
    for chunk in range(ROWS // 8):
        rows = [pl.ds(i * ROWS + chunk * 8, 8) for i in range(POPS)]
        f = [source(r) for r in rows]
        fluid = flags(pl.ds(chunk * 8, 8)) == 1
        post = relax(f)
        for i in range(POPS):
            target(rows[i], jnp.where(fluid, post[i], f[OPPOSITE[i]]))


def lanes_of(shape):
    return lax.broadcasted_iota(jnp.int32, shape, 1)


def roll_lanes(value, shift):
    shift %= 128
    return pltpu.roll(value, shift, 1) if shift else value


def pack_faces(load, store):
    lane = lanes_of((FACE_ROWS, 128))
    for face in (0, 1):
        first = 0 if face == 0 else ROWS - 2
        for k, i in enumerate(FACE_POPS[face]):
            store(face, slice(2 * k, 2 * k + 2), load(pl.ds(i * ROWS + first, 2)))
    for face in (2, 3):
        total = None
        for k, i in enumerate(FACE_POPS[face]):
            plane = load(pl.ds(i * ROWS + face - 2, EDGE, stride=2))
            plane = roll_lanes(plane, 16 * k if face == 2 else 16 * k - 112)
            total = plane if total is None else jnp.where(lane // 16 == k, plane, total)
        store(face, slice(0, FACE_ROWS), total)
    for face in (4, 5):
        total = None
        for half in range(2):
            for k, i in enumerate(FACE_POPS[face]):
                spot = 5 * half + k
                plane = load(pl.ds(i * ROWS + half * 16, 16))
                plane = roll_lanes(plane, spot if face == 4 else spot - 15)
                total = plane if total is None else jnp.where(lane % 16 == spot, plane, total)
        store(face, slice(0, FACE_ROWS), total)


def edge_mask(axis, part, row, lane):
    if axis == 0:
        return row < 2 if part > 0 else row >= ROWS - 2
    if axis == 1:
        if part > 0:
            return (row % 2 == 0) & (lane < 16)
        return (row % 2 == 1) & (lane >= 112)
    return lane % 16 == (0 if part > 0 else 15)


PAD = 8


def double_mask(parts, row, lane):
    return edge_mask(*parts[0], row, lane) & edge_mask(*parts[1], row, lane)


def stream_inside(load, wide, store):
    row = lax.broadcasted_iota(jnp.int32, (ROWS, 128), 0)
    lane = lanes_of((ROWS, 128))
    for i, (cx, cy, cz) in enumerate(VELOCITIES):
        moved = roll_lanes(load(pl.ds(i * ROWS, ROWS)), 16 * cy + cz)
        if cx or cy:
            wide[i, PAD : PAD + ROWS, :] = moved
            moved = wide[i, PAD - 2 * cx : PAD - 2 * cx + ROWS, :]
            if cy:
                start = PAD - 2 * cx - cy
                across = wide[i, start : start + ROWS, :]
                moved = jnp.where(lane >= 16 if cy > 0 else lane < 112, moved, across)
        parts = [(axis, part) for axis, part in enumerate((cx, cy, cz)) if part]
        if len(parts) == 2:
            beyond = double_mask(parts, row, lane)
            moved = jnp.where(beyond, load(pl.ds(OPPOSITE[i] * ROWS, ROWS)), moved)
        store(pl.ds(i * ROWS, ROWS), moved)


def fill_ghosts(pops, base, ghost, target):
    row = lax.broadcasted_iota(jnp.int32, (ROWS, 128), 0)
    lane = lanes_of((ROWS, 128))
    row2 = lax.broadcasted_iota(jnp.int32, (2, 128), 0)
    lane2 = lanes_of((2, 128))
    row16 = lax.broadcasted_iota(jnp.int32, (16, 128), 0)
    lane16 = lanes_of((16, 128))
    for i in pops:
        cx, cy, cz = VELOCITIES[i]
        faces = [0 if cx > 0 else 1, 2 if cy > 0 else 3, 4 if cz > 0 else 5]
        place = [FACE_POPS[face ^ 1].index(i) if part else None for face, part in zip(faces, (cx, cy, cz))]
        value = base(pl.ds(i * ROWS, ROWS))
        if cz:
            plane = ghost(faces[2], slice(0, 16))
            spot = (0 if cz > 0 else 15) + 16 * cy
            incoming = jnp.concatenate(
                [roll_lanes(plane, spot - place[2]), roll_lanes(plane, spot - 5 - place[2])], axis=0
            )
            if cx:
                incoming = pltpu.roll(incoming, 2 * cx % ROWS, 0)
            if cy:
                across = pltpu.roll(incoming, cy % ROWS, 0)
                incoming = jnp.where(lane >= 16 if cy > 0 else lane < 112, incoming, across)
            mask = edge_mask(2, cz, row, lane)
            for axis, part in ((0, cx), (1, cy)):
                if part:
                    mask = mask & jnp.logical_not(edge_mask(axis, part, row, lane))
            value = jnp.where(mask, incoming, value)
        target[pl.ds(i * ROWS, ROWS), :] = value
        if cx:
            two = roll_lanes(ghost(faces[0], slice(2 * place[0], 2 * place[0] + 2)), 16 * cy + cz)
            spots = pl.ds(i * ROWS + (0 if cx > 0 else ROWS - 2), 2)
            if cy:
                swapped = jnp.concatenate([two[1:2], two[0:1]], axis=0)
                two = jnp.where(lane2 >= 16 if cy > 0 else lane2 < 112, two, swapped)
                two = jnp.where(edge_mask(1, cy, row2, lane2), target[spots, :], two)
            if cz:
                two = jnp.where(edge_mask(2, cz, row2, lane2), target[spots, :], two)
            target[spots, :] = two
        if cy:
            plane = roll_lanes(
                ghost(faces[1], slice(0, 16)), (0 if cy > 0 else 112) - 16 * place[1] + cz
            )
            mask = lane16 < 16 if cy > 0 else lane16 >= 112
            if cx:
                plane = pltpu.roll(plane, cx % EDGE, 0)
                mask = mask & (row16 != (0 if cx > 0 else EDGE - 1))
            if cz:
                mask = mask & jnp.logical_not(edge_mask(2, cz, row16, lane16))
            spots = pl.ds(i * ROWS + (0 if cy > 0 else 1), EDGE, stride=2)
            target[spots, :] = jnp.where(mask, plane, target[spots, :])


def bounce_face(face, load, new_load, store):
    row = lax.broadcasted_iota(jnp.int32, (ROWS, 128), 0)
    lane = lanes_of((ROWS, 128))
    part = -1 if face % 2 else 1
    mask = edge_mask(face // 2, part, row, lane)
    for i in FACE_POPS[face ^ 1]:
        rows = pl.ds(i * ROWS, ROWS)
        store(rows, jnp.where(mask, load(pl.ds(OPPOSITE[i] * ROWS, ROWS)), new_load(rows)))


def cycle_offset(place, cycle):
    offset = lax.shift_right_arithmetic(place, 2) - lax.axis_index("blocks")
    offset = jnp.where(offset > REACH, offset - cycle, offset)
    return jnp.where(offset < -REACH, offset + cycle, offset)


def pack_kernel(moves, pdfs, *outs):
    values = [sent_offset(kind)[0] for kind in BLOCK_ORDER] + [0]
    for out, value in zip(outs, values):
        source = jnp.int32(0)
        for j in range(BLK_DEV):
            source = jnp.where(moves[j] == value, j, source)
        out[...] = pdfs[pl.ds(source, BLOCK_ROWS, stride=BLK_DEV), :]


def index_kernel(cycle, neighbours, sends, receives, ranks):
    for n in range(FACES):
        sends[n] = 0
    for n in range((len(OFFSETS) + 1) * FACES):
        ranks[n] = -1
    counts = [jnp.int32(0) for _ in OFFSETS]
    for n in range(FACES):
        place = neighbours[n // 6, n % 6]
        offset = cycle_offset(place, cycle)
        across = (place & 3) * 6 + (n % 6 ^ 1)
        receives[n] = jnp.where(place < 0, -1, FACES + across)
        for o, value in enumerate(OFFSETS):
            mine = (place >= 0) & (offset == value)
            at = jnp.where(mine, o, len(OFFSETS)) * FACES
            ranks[at + across] = n

            @pl.when(mine & (counts[o] < PEER_FACES))
            def _(o=o, count=counts[o]):
                sends[o * PEER_FACES + count] = n

            counts[o] = counts[o] + mine.astype(jnp.int32)
    for o in range(len(OFFSETS)):
        seen = jnp.int32(0)
        for key in range(FACES):
            face = ranks[o * FACES + key]
            found = face >= 0

            @pl.when(found)
            def _(o=o, seen=seen, face=face):
                receives[face] = o * PEER_FACES + jnp.minimum(seen, PEER_FACES - 1)

            seen = seen + found.astype(jnp.int32)


ROUTES = {
    "p2": lambda i: i + 2,
    "m2": lambda i: i - 2,
    "p1": lambda i: i + 1,
    "m1": lambda i: i - 1,
    "x": lambda i: i + 1 if i % 2 else i - 1,
    "a": lambda i: i ^ 1,
}
BLOCK_ORDER = ('p2', 'x', 'm2', 'a')
FACE_ORDER = ('p2', 'x', 'm2', 'a')


def sent_offset(kind):
    core = lax.axis_index("blocks") & 1
    to = {"p2": 2, "m2": -2, "p1": 1, "m1": -1, "x": 2 * core - 1, "a": 1 - 2 * core}[kind]
    return to, -to if kind in ("x", "a") else to


def offset_place(offset):
    return offset + REACH - (offset > 0) if isinstance(offset, int) else (offset + 3) >> 1


def send_faces(sends, faces, outs):
    for kind, out in zip(FACE_ORDER, outs):
        o = offset_place(sent_offset(kind)[0])
        for r in range(PEER_FACES):
            out[r * FACE_ROWS : (r + 1) * FACE_ROWS, :] = faces[sends[o * PEER_FACES + r]]


def pack_block(post, faces, b):
    def store(face, rows, value):
        faces[b * 6 + face, rows, :] = value

    pack_faces(lambda rows: post[b, rows, :], store)


def flags_of(flags, b):
    return lambda rows: flags[pl.ds(BLK_DEV * rows.start + b, rows.size, stride=BLK_DEV), :]


def first_kernel(moves, sends, flags, *refs):
    arrived, (post, faces), outs, new = refs[:5], refs[5:7], refs[7:-1], refs[-1]
    values = [sent_offset(kind)[1] for kind in BLOCK_ORDER] + [0]
    for n, source in enumerate(arrived):
        new[n] = source[...]
    sources = []
    for j in range(BLK_DEV):
        source = jnp.int32(0)
        for n, value in enumerate(values):
            source = jnp.where(moves[j] == value, n, source)
        sources.append(source)

    @pl.loop(0, BLK_DEV, unroll=BLK_DEV)
    def _(b):
        source = jnp.int32(0)
        for j in range(BLK_DEV):
            source = jnp.where(moves[BLK_DEV + j] == b, sources[j], source)

        def store(rows, value):
            post[b, rows, :] = value

        collide_block(lambda r: new[source, r, :], flags_of(flags, b), store)
        pack_block(post, faces, b)

    send_faces(sends, faces, outs)


def fill_pool(pool, arrived, own):
    for kind, source in zip(FACE_ORDER, arrived):
        o = offset_place(-sent_offset(kind)[1])
        for r in range(PEER_FACES):
            pool[o * PEER_FACES + r] = source[r * FACE_ROWS : (r + 1) * FACE_ROWS, :]
    pool[FACES:] = own[...]


def inside_kernel(post, new, wide):
    @pl.loop(0, BLK_DEV, unroll=BLK_DEV)
    def _(b):
        def store(rows, value):
            new[b, rows, :] = value

        stream_inside(lambda rows: post[b, rows, :], wide, store)


def fill_block(b, pops, receives, inside, pool, new):
    spots = [jnp.maximum(receives[b * 6 + face], 0) for face in range(6)]
    fill_ghosts(
        pops,
        lambda rows: inside[b, rows, :],
        lambda face, rows: pool[spots[face], rows, :],
        new,
    )


def bounce_block(b, receives, post, new):
    def store(rows, value):
        new[rows, :] = value

    for face in range(6):

        @pl.when(receives[b * 6 + face] < 0)
        def _(face=face):
            bounce_face(face, lambda rows: post[b, rows, :], lambda rows: new[rows, :], store)


def step_kernel(sends, receives, flags, post, inside, own, *refs):
    arrived, (post_out, faces), outs, (pool, new) = refs[:4], refs[4:6], refs[6:10], refs[10:]
    fill_pool(pool, arrived, own)

    @pl.loop(0, BLK_DEV, unroll=BLK_DEV)
    def _(b):
        fill_block(b, range(POPS), receives, inside, pool, new)
        bounce_block(b, receives, post, new)

        def store(rows, value):
            post_out[b, rows, :] = value

        collide_block(lambda r: new[r, :], flags_of(flags, b), store)
        pack_block(post_out, faces, b)

    send_faces(sends, faces, outs)


def last_kernel(receives, post, inside, own, *refs):
    arrived, out, (pool, new, whole, sem) = refs[:4], refs[4], refs[5:]
    fill_pool(pool, arrived, own)

    def store_out(i):
        for b in range(BLK_DEV):
            whole[pl.ds(i * ROWS * BLK_DEV + b, ROWS, stride=BLK_DEV), :] = new[
                b, i * ROWS : (i + 1) * ROWS, :
            ]
        rows = pl.ds(i * ROWS * BLK_DEV, ROWS * BLK_DEV)
        copy = pltpu.make_async_copy(whole.at[rows, :], out.at[rows, :], sem.at[i])
        copy.start()
        return copy

    copies = []
    for i in range(POPS):
        for b in range(BLK_DEV):
            fill_block(b, [i], receives, inside, pool, new.at[b])
        copies.append(store_out(i))
    for copy in copies:
        copy.wait()
    least = receives[0]
    for n in range(1, FACES):
        least = jnp.minimum(least, receives[n])

    @pl.when(least < 0)
    def _():
        for b in range(BLK_DEV):
            bounce_block(b, receives, post, new.at[b])
        for copy in [store_out(i) for i in range(POPS)]:
            copy.wait()


SMEM = pl.BlockSpec(memory_space=pltpu.SMEM)
VMEM = pl.BlockSpec(memory_space=pltpu.VMEM)
HBM = pl.BlockSpec(memory_space=pltpu.HBM)
BLOCK = jax.ShapeDtypeStruct((BLOCK_ROWS, 128), jnp.float32)
POST = jax.ShapeDtypeStruct((BLK_DEV, BLOCK_ROWS, 128), jnp.float32)
OWN = jax.ShapeDtypeStruct((FACES, FACE_ROWS, 128), jnp.float32)
SENT = jax.ShapeDtypeStruct((PEER_FACES * FACE_ROWS, 128), jnp.float32)
POOL = pltpu.VMEM((2 * FACES, FACE_ROWS, 128), jnp.float32)
WIDE = pltpu.VMEM((POPS, ROWS + 2 * PAD, 128), jnp.float32)
NEW = pltpu.VMEM((BLOCK_ROWS, 128), jnp.float32)


def call(
    kernel, in_specs, out_shapes, out_specs, scratch=(), flops=0, bytes_accessed=0
):
    return pl.pallas_call(
        kernel,
        in_specs=in_specs,
        out_shape=out_shapes,
        out_specs=out_specs,
        scratch_shapes=list(scratch),
        compiler_params=pltpu.CompilerParams(vmem_limit_bytes=VMEM_BYTES),
        cost_estimate=pl.CostEstimate(
            flops=flops, bytes_accessed=bytes_accessed, transcendentals=0
        ),
    )


def exchange(buffers, order, cycle):
    return [
        lax.ppermute(value, "blocks", [(i, ROUTES[kind](i) % cycle) for i in range(cycle)])
        for value, kind in zip(buffers, order)
    ]


def body(pdfs, plan, neighbours, flags):
    cycle = lax.axis_size("blocks")
    size = 4 * pdfs.size
    rows = pdfs.transpose(1, 0, 2).reshape(POPS, BLK_DEV, ROWS, 128)
    rows = rows.transpose(0, 2, 1, 3).reshape(BLK_DEV * BLOCK_ROWS, 128)
    moves = jnp.concatenate([cycle_offset(plan, cycle), plan & 3])
    sent = call(
        pack_kernel, [SMEM, VMEM], [BLOCK] * 5, [VMEM] * 5, bytes_accessed=2 * size
    )(moves, rows)
    arrived = exchange(sent, BLOCK_ORDER, cycle) + [sent[4]]
    table = jax.ShapeDtypeStruct((FACES,), jnp.int32)
    sends, receives = call(
        functools.partial(index_kernel, cycle), [SMEM], [table] * 2, [SMEM] * 2,
        [pltpu.SMEM(((len(OFFSETS) + 1) * FACES,), jnp.int32)], bytes_accessed=1000,
    )(neighbours)
    cells = flags.reshape(BLK_DEV, ROWS, 128).transpose(1, 0, 2).reshape(BLK_DEV * ROWS, 128)
    outs = dict(
        out_shapes=[POST, OWN] + [SENT] * 4, out_specs=[VMEM] * 6,
        flops=300 * pdfs.size // POPS, bytes_accessed=2 * size,
    )
    inside = call(inside_kernel, [VMEM], POST, VMEM, [WIDE], bytes_accessed=2 * size)
    post, own, *faces = call(
        first_kernel, [SMEM, SMEM] + [VMEM] * 6,
        scratch=[pltpu.VMEM((BLK_DEV + 1, BLOCK_ROWS, 128), jnp.float32)], **outs
    )(moves, sends, cells, *arrived)
    for _ in range(STEPS - 1):
        came = exchange(faces, FACE_ORDER, cycle)
        post, own, *faces = call(
            step_kernel, [SMEM, SMEM] + [VMEM] * 8, scratch=[POOL, NEW], **outs
        )(sends, receives, cells, post, inside(post), own, *came)
    came = exchange(faces, FACE_ORDER, cycle)
    whole = (BLK_DEV * BLOCK_ROWS, 128)
    out = call(
        last_kernel, [SMEM] + [VMEM] * 7,
        jax.ShapeDtypeStruct(whole, jnp.float32), HBM,
        [POOL, pltpu.VMEM(POST.shape, jnp.float32), pltpu.VMEM(whole, jnp.float32),
         pltpu.SemaphoreType.DMA((POPS,))],
        bytes_accessed=2 * size,
    )(receives, post, inside(post), own, *came)
    out = out.reshape(POPS, ROWS, BLK_DEV, 128).transpose(2, 0, 1, 3)
    return out.reshape(pdfs.shape)


def solution(mesh):
    placed = (P("blocks", None, None), P("blocks"), P("blocks", None), P("blocks", None))
    return jax.shard_map(
        body, mesh=mesh, in_specs=placed, out_specs=P("blocks", None, None), check_vma=False
    )
```

```python
import functools

import jax
import jax.numpy as jnp
import numpy as np
from jax import lax
from jax.experimental import pallas as pl
from jax.experimental.pallas import tpu as pltpu
from jax.sharding import PartitionSpec as P

EDGE = 16
BLK_DEV = 4
REACH = 2
STEPS = 3
POPS = 19
ROWS = EDGE**3 // 128
BLOCK_ROWS = POPS * ROWS
FACE_ROWS = 16
FACES = 6 * BLK_DEV
PEER_FACES = 6
OFFSETS = (-2, -1, 1, 2)
REST_DENSITY = 36.0
SHEAR_RATE = 1.6
VMEM_BYTES = 24 * 1024 * 1024

VELOCITIES = [
    (0, 0, 0), (1, 0, 0), (-1, 0, 0), (0, 1, 0), (0, -1, 0), (0, 0, 1), (0, 0, -1),
    (1, 1, 0), (-1, -1, 0), (1, -1, 0), (-1, 1, 0), (1, 0, 1), (-1, 0, -1), (1, 0, -1),
    (-1, 0, 1), (0, 1, 1), (0, -1, -1), (0, 1, -1), (0, -1, 1),
]
OPPOSITE = [VELOCITIES.index((-a, -b, -c)) for a, b, c in VELOCITIES]
FACE_POPS = [
    [i for i, c in enumerate(VELOCITIES) if c[face // 2] == (1 if face % 2 else -1)]
    for face in range(6)
]
WEIGHTS = [1.0 / 3.0] + [1.0 / 18.0] * 6 + [1.0 / 36.0] * 12


def moment_constants():
    c = np.array(VELOCITIES) * 1.0
    x, y, z = c[:, 0], c[:, 1], c[:, 2]
    s = x * x + y * y + z * z
    rows = {
        "e": 19 * s - 30,
        "eps": (21 * s * s - 53 * s + 24) / 2,
        "q": (5 * s - 9) * x,
        "pxx": 3 * x * x - s,
        "pixx": (3 * s - 5) * (3 * x * x - s),
        "pww": y * y - z * z,
        "piww": (3 * s - 5) * (y * y - z * z),
        "pxy": x * y,
        "m": x * (y * y - z * z),
    }
    rates = {
        "e": 1.19, "eps": 1.4, "q": 1.2, "pxx": SHEAR_RATE, "pixx": 1.4, "pww": SHEAR_RATE,
        "piww": 1.4, "pxy": SHEAR_RATE, "m": 1.98,
    }
    scale = {k: float(rates[k] / np.sum(rows[k] ** 2)) for k in rows}
    w = np.array(WEIGHTS)

    def of(row, term):
        return float(np.sum(rows[row] * w * term))

    square = [(4.5 * x * x - 1.5) / REST_DENSITY, (4.5 * y * y - 1.5) / REST_DENSITY,
              (4.5 * z * z - 1.5) / REST_DENSITY]
    terms = {
        "e_rho": of("e", 1.0), "eps_rho": of("eps", 1.0), "q_j": of("q", 3 * x),
        "pxy_jj": of("pxy", 9.0 * x * y / REST_DENSITY),
    }
    for name in ("e", "eps", "pxx", "pixx", "pww", "piww"):
        terms[name] = [of(name, t) for t in square]
    return scale, terms


SCALE, TERMS = moment_constants()


def relax(f):
    ex, ey, ez = f[1] + f[2], f[3] + f[4], f[5] + f[6]
    ox, oy, oz = f[1] - f[2], f[3] - f[4], f[5] - f[6]
    a, oa = f[7] + f[8], f[7] - f[8]
    b, ob = f[9] + f[10], f[9] - f[10]
    c, oc = f[11] + f[12], f[11] - f[12]
    d, od = f[13] + f[14], f[13] - f[14]
    g, og = f[15] + f[16], f[15] - f[16]
    h, oh = f[17] + f[18], f[17] - f[18]
    sxy, sxz, syz = a + b, c + d, g + h
    axial = ex + (ey + ez)
    diagonal = sxy + (sxz + syz)
    rho = f[0] + (axial + diagonal)
    xy_x, xz_x = oa + ob, oc + od
    xy_y, yz_y = oa - ob, og + oh
    xz_z, yz_z = oc - od, og - oh
    dx, dy, dz = xy_x + xz_x, xy_y + yz_y, xz_z + yz_z
    jx, jy, jz = ox + dx, oy + dy, oz + dz
    xx, yy, zz = jx * jx, jy * jy, jz * jz

    def even(name, value):
        k = TERMS[name]
        if abs(k[1] - k[2]) < 1e-12 and abs(k[0] - k[1]) < 1e-12:
            quad = (k[0] * SCALE[name]) * (xx + yy + zz)
        elif abs(k[0]) < 1e-12:
            quad = (k[1] * SCALE[name]) * (yy - zz)
        else:
            quad = (k[0] * SCALE[name]) * xx + (k[1] * SCALE[name]) * (yy + zz)
        return SCALE[name] * value - quad

    t_e = even("e", 8.0 * diagonal - 30.0 * f[0] - 11.0 * axial - TERMS["e_rho"] * rho)
    t_eps = even("eps", 12.0 * f[0] - 4.0 * axial + diagonal - TERMS["eps_rho"] * rho)
    p_axis = 2.0 * ex - (ey + ez)
    p_diag = (sxy + sxz) - 2.0 * syz
    w_axis = ey - ez
    w_diag = sxy - sxz
    t_pxx = even("pxx", p_axis + p_diag)
    t_pixx = even("pixx", p_diag - 2.0 * p_axis)
    t_pww = even("pww", w_axis + w_diag)
    t_piww = even("piww", w_diag - 2.0 * w_axis)
    k_p = TERMS["pxy_jj"]
    t_xy = SCALE["pxy"] * ((a - b) - k_p * (jx * jy))
    t_yz = SCALE["pxy"] * ((g - h) - k_p * (jy * jz))
    t_xz = SCALE["pxy"] * ((c - d) - k_p * (jx * jz))
    k_q = TERMS["q_j"]
    t_qx = SCALE["q"] * (dx - 4.0 * ox - k_q * jx)
    t_qy = SCALE["q"] * (dy - 4.0 * oy - k_q * jy)
    t_qz = SCALE["q"] * (dz - 4.0 * oz - k_q * jz)
    t_mx = SCALE["m"] * (xy_x - xz_x)
    t_my = SCALE["m"] * (yz_y - xy_y)
    t_mz = SCALE["m"] * (xz_z - yz_z)

    base_axis = -11.0 * t_e - 4.0 * t_eps
    base_diag = 8.0 * t_e + t_eps
    p1 = t_pxx - 2.0 * t_pixx
    w1 = t_pww - 2.0 * t_piww
    p2 = t_pxx + t_pixx
    w2 = t_pww + t_piww
    kx = base_axis + 2.0 * p1
    k_yz = base_axis - p1
    ky, kz = k_yz + w1, k_yz - w1
    near = base_diag + p2
    kxy, kxz, kyz = near + w2, near - w2, base_diag - 2.0 * p2
    qx4, qy4, qz4 = -4.0 * t_qx, -4.0 * t_qy, -4.0 * t_qz
    xp, xm = t_qx + t_mx, t_qx - t_mx
    yp, ym = t_qy + t_my, t_qy - t_my
    zp, zm = t_qz + t_mz, t_qz - t_mz
    pairs = [
        (kx, qx4), (ky, qy4), (kz, qz4),
        (kxy + t_xy, xp + ym), (kxy - t_xy, xp - ym),
        (kxz + t_xz, xm + zp), (kxz - t_xz, xm - zp),
        (kyz + t_yz, yp + zm), (kyz - t_yz, yp - zm),
    ]
    out = [f[0] - (12.0 * t_eps - 30.0 * t_e)]
    for n, (same, odd) in enumerate(pairs):
        out.append(f[2 * n + 1] - (same + odd))
        out.append(f[2 * n + 2] - (same - odd))
    return out


def collide_block(source, flags, target):
    for chunk in range(ROWS // 8):
        rows = [pl.ds(i * ROWS + chunk * 8, 8) for i in range(POPS)]
        f = [source(r) for r in rows]
        fluid = flags(pl.ds(chunk * 8, 8)) == 1
        post = relax(f)
        for i in range(POPS):
            target(rows[i], jnp.where(fluid, post[i], f[OPPOSITE[i]]))


def lanes_of(shape):
    return lax.broadcasted_iota(jnp.int32, shape, 1)


def roll_lanes(value, shift):
    shift %= 128
    return pltpu.roll(value, shift, 1) if shift else value


def pack_faces(load, store):
    lane = lanes_of((FACE_ROWS, 128))
    for face in (0, 1):
        first = 0 if face == 0 else ROWS - 2
        for k, i in enumerate(FACE_POPS[face]):
            store(face, slice(2 * k, 2 * k + 2), load(pl.ds(i * ROWS + first, 2)))
    for face in (2, 3):
        total = None
        for k, i in enumerate(FACE_POPS[face]):
            plane = load(pl.ds(i * ROWS + face - 2, EDGE, stride=2))
            plane = roll_lanes(plane, 16 * k if face == 2 else 16 * k - 112)
            total = plane if total is None else jnp.where(lane // 16 == k, plane, total)
        store(face, slice(0, FACE_ROWS), total)
    for face in (4, 5):
        total = None
        for half in range(2):
            for k, i in enumerate(FACE_POPS[face]):
                spot = 5 * half + k
                plane = load(pl.ds(i * ROWS + half * 16, 16))
                plane = roll_lanes(plane, spot if face == 4 else spot - 15)
                total = plane if total is None else jnp.where(lane % 16 == spot, plane, total)
        store(face, slice(0, FACE_ROWS), total)


def edge_mask(axis, part, row, lane):
    if axis == 0:
        return row < 2 if part > 0 else row >= ROWS - 2
    if axis == 1:
        if part > 0:
            return (row % 2 == 0) & (lane < 16)
        return (row % 2 == 1) & (lane >= 112)
    return lane % 16 == (0 if part > 0 else 15)


PAD = 8


def double_mask(parts, row, lane):
    return edge_mask(*parts[0], row, lane) & edge_mask(*parts[1], row, lane)


def stream_inside(load, wide, store):
    row = lax.broadcasted_iota(jnp.int32, (ROWS, 128), 0)
    lane = lanes_of((ROWS, 128))
    for i, (cx, cy, cz) in enumerate(VELOCITIES):
        moved = roll_lanes(load(pl.ds(i * ROWS, ROWS)), 16 * cy + cz)
        if cx or cy:
            wide[i, PAD : PAD + ROWS, :] = moved
            moved = wide[i, PAD - 2 * cx : PAD - 2 * cx + ROWS, :]
            if cy:
                start = PAD - 2 * cx - cy
                across = wide[i, start : start + ROWS, :]
                moved = jnp.where(lane >= 16 if cy > 0 else lane < 112, moved, across)
        parts = [(axis, part) for axis, part in enumerate((cx, cy, cz)) if part]
        if len(parts) == 2:
            beyond = double_mask(parts, row, lane)
            moved = jnp.where(beyond, load(pl.ds(OPPOSITE[i] * ROWS, ROWS)), moved)
        store(pl.ds(i * ROWS, ROWS), moved)


def fill_ghosts(pops, base, ghost, target):
    row = lax.broadcasted_iota(jnp.int32, (ROWS, 128), 0)
    lane = lanes_of((ROWS, 128))
    row2 = lax.broadcasted_iota(jnp.int32, (2, 128), 0)
    lane2 = lanes_of((2, 128))
    row16 = lax.broadcasted_iota(jnp.int32, (16, 128), 0)
    lane16 = lanes_of((16, 128))
    for i in pops:
        cx, cy, cz = VELOCITIES[i]
        faces = [0 if cx > 0 else 1, 2 if cy > 0 else 3, 4 if cz > 0 else 5]
        place = [FACE_POPS[face ^ 1].index(i) if part else None for face, part in zip(faces, (cx, cy, cz))]
        value = base(pl.ds(i * ROWS, ROWS))
        if cz:
            plane = ghost(faces[2], slice(0, 16))
            spot = (0 if cz > 0 else 15) + 16 * cy
            incoming = jnp.concatenate(
                [roll_lanes(plane, spot - place[2]), roll_lanes(plane, spot - 5 - place[2])], axis=0
            )
            if cx:
                incoming = pltpu.roll(incoming, 2 * cx % ROWS, 0)
            if cy:
                across = pltpu.roll(incoming, cy % ROWS, 0)
                incoming = jnp.where(lane >= 16 if cy > 0 else lane < 112, incoming, across)
            mask = edge_mask(2, cz, row, lane)
            for axis, part in ((0, cx), (1, cy)):
                if part:
                    mask = mask & jnp.logical_not(edge_mask(axis, part, row, lane))
            value = jnp.where(mask, incoming, value)
        target[pl.ds(i * ROWS, ROWS), :] = value
        if cx:
            two = roll_lanes(ghost(faces[0], slice(2 * place[0], 2 * place[0] + 2)), 16 * cy + cz)
            spots = pl.ds(i * ROWS + (0 if cx > 0 else ROWS - 2), 2)
            if cy:
                swapped = jnp.concatenate([two[1:2], two[0:1]], axis=0)
                two = jnp.where(lane2 >= 16 if cy > 0 else lane2 < 112, two, swapped)
                two = jnp.where(edge_mask(1, cy, row2, lane2), target[spots, :], two)
            if cz:
                two = jnp.where(edge_mask(2, cz, row2, lane2), target[spots, :], two)
            target[spots, :] = two
        if cy:
            plane = roll_lanes(
                ghost(faces[1], slice(0, 16)), (0 if cy > 0 else 112) - 16 * place[1] + cz
            )
            mask = lane16 < 16 if cy > 0 else lane16 >= 112
            if cx:
                plane = pltpu.roll(plane, cx % EDGE, 0)
                mask = mask & (row16 != (0 if cx > 0 else EDGE - 1))
            if cz:
                mask = mask & jnp.logical_not(edge_mask(2, cz, row16, lane16))
            spots = pl.ds(i * ROWS + (0 if cy > 0 else 1), EDGE, stride=2)
            target[spots, :] = jnp.where(mask, plane, target[spots, :])


def bounce_face(face, load, new_load, store):
    row = lax.broadcasted_iota(jnp.int32, (ROWS, 128), 0)
    lane = lanes_of((ROWS, 128))
    part = -1 if face % 2 else 1
    mask = edge_mask(face // 2, part, row, lane)
    for i in FACE_POPS[face ^ 1]:
        rows = pl.ds(i * ROWS, ROWS)
        store(rows, jnp.where(mask, load(pl.ds(OPPOSITE[i] * ROWS, ROWS)), new_load(rows)))


def cycle_offset(place, cycle):
    offset = lax.shift_right_arithmetic(place, 2) - lax.axis_index("blocks")
    offset = jnp.where(offset > REACH, offset - cycle, offset)
    return jnp.where(offset < -REACH, offset + cycle, offset)


def pack_kernel(kinds, moves, pdfs, *outs):
    values = [sent_offset(kind)[0] if kind else 0 for kind in kinds]
    for out, value in zip(outs, values):
        source = jnp.int32(0)
        for j in range(BLK_DEV):
            source = jnp.where(moves[j] == value, j, source)
        out[...] = pdfs[pl.ds(source, BLOCK_ROWS, stride=BLK_DEV), :]


def index_kernel(cycle, neighbours, sends, receives, ranks):
    for n in range(FACES):
        sends[n] = 0
    for n in range((len(OFFSETS) + 1) * FACES):
        ranks[n] = -1
    counts = [jnp.int32(0) for _ in OFFSETS]
    for n in range(FACES):
        place = neighbours[n // 6, n % 6]
        offset = cycle_offset(place, cycle)
        across = (place & 3) * 6 + (n % 6 ^ 1)
        receives[n] = jnp.where(place < 0, -1, FACES + across)
        for o, value in enumerate(OFFSETS):
            mine = (place >= 0) & (offset == value)
            at = jnp.where(mine, o, len(OFFSETS)) * FACES
            ranks[at + across] = n

            @pl.when(mine & (counts[o] < PEER_FACES))
            def _(o=o, count=counts[o]):
                sends[o * PEER_FACES + count] = n

            counts[o] = counts[o] + mine.astype(jnp.int32)
    for o in range(len(OFFSETS)):
        seen = jnp.int32(0)
        for key in range(FACES):
            face = ranks[o * FACES + key]
            found = face >= 0

            @pl.when(found)
            def _(o=o, seen=seen, face=face):
                receives[face] = o * PEER_FACES + jnp.minimum(seen, PEER_FACES - 1)

            seen = seen + found.astype(jnp.int32)


ROUTES = {
    "p2": lambda i: i + 2,
    "m2": lambda i: i - 2,
    "p1": lambda i: i + 1,
    "m1": lambda i: i - 1,
    "x": lambda i: i + 1 if i % 2 else i - 1,
    "a": lambda i: i ^ 1,
}
BLOCK_ORDER = ('p2', 'x', 'm2', 'a')
FACE_ORDER = ('p2', 'x', 'm2', 'a')


def sent_offset(kind):
    core = lax.axis_index("blocks") & 1
    to = {"p2": 2, "m2": -2, "p1": 1, "m1": -1, "x": 2 * core - 1, "a": 1 - 2 * core}[kind]
    return to, -to if kind in ("x", "a") else to


def offset_place(offset):
    return offset + REACH - (offset > 0) if isinstance(offset, int) else (offset + 3) >> 1


def send_faces(sends, faces, outs):
    for kind, out in zip(FACE_ORDER, outs):
        o = offset_place(sent_offset(kind)[0])
        for r in range(PEER_FACES):
            out[r * FACE_ROWS : (r + 1) * FACE_ROWS, :] = faces[sends[o * PEER_FACES + r]]


def pack_block(post, faces, b):
    def store(face, rows, value):
        faces[b * 6 + face, rows, :] = value

    pack_faces(lambda rows: post[b, rows, :], store)


def flags_of(flags, b):
    return lambda rows: flags[pl.ds(BLK_DEV * rows.start + b, rows.size, stride=BLK_DEV), :]


def first_kernel(moves, sends, flags, *refs):
    arrived, (post, faces), outs, new = refs[:5], refs[5:7], refs[7:-1], refs[-1]
    values = [sent_offset(kind)[1] for kind in BLOCK_ORDER] + [0]
    for n, source in enumerate(arrived):
        new[n] = source[...]
    sources = []
    for j in range(BLK_DEV):
        source = jnp.int32(0)
        for n, value in enumerate(values):
            source = jnp.where(moves[j] == value, n, source)
        sources.append(source)

    @pl.loop(0, BLK_DEV, unroll=BLK_DEV)
    def _(b):
        source = jnp.int32(0)
        for j in range(BLK_DEV):
            source = jnp.where(moves[BLK_DEV + j] == b, sources[j], source)

        def store(rows, value):
            post[b, rows, :] = value

        collide_block(lambda r: new[source, r, :], flags_of(flags, b), store)
        pack_block(post, faces, b)

    send_faces(sends, faces, outs)


def fill_pool(pool, receives, arrived, own):
    for kind, source in zip(FACE_ORDER, arrived):
        o = offset_place(-sent_offset(kind)[1])
        for r in range(PEER_FACES):
            pool[o * PEER_FACES + r] = source[r * FACE_ROWS : (r + 1) * FACE_ROWS, :]
    most = receives[0]
    for n in range(1, FACES):
        most = jnp.maximum(most, receives[n])

    @pl.when(most >= FACES)
    def _():
        pool[FACES:] = own[...]


def inside_kernel(post, new, wide):
    @pl.loop(0, BLK_DEV, unroll=BLK_DEV)
    def _(b):
        def store(rows, value):
            new[b, rows, :] = value

        stream_inside(lambda rows: post[b, rows, :], wide, store)


def fill_block(b, pops, receives, inside, pool, new):
    spots = [jnp.maximum(receives[b * 6 + face], 0) for face in range(6)]
    fill_ghosts(
        pops,
        lambda rows: inside[b, rows, :],
        lambda face, rows: pool[spots[face], rows, :],
        new,
    )


def bounce_block(b, receives, post, new):
    def store(rows, value):
        new[rows, :] = value

    for face in range(6):

        @pl.when(receives[b * 6 + face] < 0)
        def _(face=face):
            bounce_face(face, lambda rows: post[b, rows, :], lambda rows: new[rows, :], store)


def step_kernel(sends, receives, flags, post, inside, own, *refs):
    arrived, (post_out, faces), outs, (pool, new) = refs[:4], refs[4:6], refs[6:10], refs[10:]
    fill_pool(pool, receives, arrived, own)

    @pl.loop(0, BLK_DEV, unroll=BLK_DEV)
    def _(b):
        fill_block(b, range(POPS), receives, inside, pool, new)
        bounce_block(b, receives, post, new)

        def store(rows, value):
            post_out[b, rows, :] = value

        collide_block(lambda r: new[r, :], flags_of(flags, b), store)
        pack_block(post_out, faces, b)

    send_faces(sends, faces, outs)


def last_kernel(receives, post, inside, own, *refs):
    arrived, out, (pool, new, whole, sem) = refs[:4], refs[4], refs[5:]
    fill_pool(pool, receives, arrived, own)

    def store_out(i):
        for b in range(BLK_DEV):
            whole[pl.ds(i * ROWS * BLK_DEV + b, ROWS, stride=BLK_DEV), :] = new[
                b, i * ROWS : (i + 1) * ROWS, :
            ]
        rows = pl.ds(i * ROWS * BLK_DEV, ROWS * BLK_DEV)
        copy = pltpu.make_async_copy(whole.at[rows, :], out.at[rows, :], sem.at[i])
        copy.start()
        return copy

    copies = []
    for i in range(POPS):
        for b in range(BLK_DEV):
            fill_block(b, [i], receives, inside, pool, new.at[b])
        copies.append(store_out(i))
    for copy in copies:
        copy.wait()
    least = receives[0]
    for n in range(1, FACES):
        least = jnp.minimum(least, receives[n])

    @pl.when(least < 0)
    def _():
        for b in range(BLK_DEV):
            bounce_block(b, receives, post, new.at[b])
        for copy in [store_out(i) for i in range(POPS)]:
            copy.wait()


SMEM = pl.BlockSpec(memory_space=pltpu.SMEM)
VMEM = pl.BlockSpec(memory_space=pltpu.VMEM)
HBM = pl.BlockSpec(memory_space=pltpu.HBM)
BLOCK = jax.ShapeDtypeStruct((BLOCK_ROWS, 128), jnp.float32)
POST = jax.ShapeDtypeStruct((BLK_DEV, BLOCK_ROWS, 128), jnp.float32)
OWN = jax.ShapeDtypeStruct((FACES, FACE_ROWS, 128), jnp.float32)
SENT = jax.ShapeDtypeStruct((PEER_FACES * FACE_ROWS, 128), jnp.float32)
POOL = pltpu.VMEM((2 * FACES, FACE_ROWS, 128), jnp.float32)
WIDE = pltpu.VMEM((POPS, ROWS + 2 * PAD, 128), jnp.float32)
NEW = pltpu.VMEM((BLOCK_ROWS, 128), jnp.float32)


def call(
    kernel, in_specs, out_shapes, out_specs, scratch=(), flops=0, bytes_accessed=0
):
    return pl.pallas_call(
        kernel,
        in_specs=in_specs,
        out_shape=out_shapes,
        out_specs=out_specs,
        scratch_shapes=list(scratch),
        compiler_params=pltpu.CompilerParams(vmem_limit_bytes=VMEM_BYTES),
        cost_estimate=pl.CostEstimate(
            flops=flops, bytes_accessed=bytes_accessed, transcendentals=0
        ),
    )


def exchange(buffers, order, cycle):
    return [
        lax.ppermute(value, "blocks", [(i, ROUTES[kind](i) % cycle) for i in range(cycle)])
        for value, kind in zip(buffers, order)
    ]


def body(pdfs, plan, neighbours, flags):
    cycle = lax.axis_size("blocks")
    size = 4 * pdfs.size
    rows = pdfs.transpose(1, 0, 2).reshape(POPS, BLK_DEV, ROWS, 128)
    rows = rows.transpose(0, 2, 1, 3).reshape(BLK_DEV * BLOCK_ROWS, 128)
    moves = jnp.concatenate([cycle_offset(plan, cycle), plan & 3])
    sent = call(
        functools.partial(pack_kernel, BLOCK_ORDER), [SMEM, VMEM], [BLOCK] * 4, [VMEM] * 4,
        bytes_accessed=2 * size,
    )(moves, rows)
    kept = call(
        functools.partial(pack_kernel, (None,)), [SMEM, VMEM], [BLOCK], [VMEM],
        bytes_accessed=2 * size,
    )(moves, rows)
    arrived = exchange(sent, BLOCK_ORDER, cycle) + list(kept)
    table = jax.ShapeDtypeStruct((FACES,), jnp.int32)
    sends, receives = call(
        functools.partial(index_kernel, cycle), [SMEM], [table] * 2, [SMEM] * 2,
        [pltpu.SMEM(((len(OFFSETS) + 1) * FACES,), jnp.int32)], bytes_accessed=1000,
    )(neighbours)
    cells = flags.reshape(BLK_DEV, ROWS, 128).transpose(1, 0, 2).reshape(BLK_DEV * ROWS, 128)
    outs = dict(
        out_shapes=[POST, OWN] + [SENT] * 4, out_specs=[VMEM] * 6,
        flops=300 * pdfs.size // POPS, bytes_accessed=2 * size,
    )
    inside = call(inside_kernel, [VMEM], POST, VMEM, [WIDE], bytes_accessed=2 * size)
    post, own, *faces = call(
        first_kernel, [SMEM, SMEM] + [VMEM] * 6,
        scratch=[pltpu.VMEM((BLK_DEV + 1, BLOCK_ROWS, 128), jnp.float32)], **outs
    )(moves, sends, cells, *arrived)
    for _ in range(STEPS - 1):
        came = exchange(faces, FACE_ORDER, cycle)
        post, own, *faces = call(
            step_kernel, [SMEM, SMEM] + [VMEM] * 8, scratch=[POOL, NEW], **outs
        )(sends, receives, cells, post, inside(post), own, *came)
    came = exchange(faces, FACE_ORDER, cycle)
    whole = (BLK_DEV * BLOCK_ROWS, 128)
    out = call(
        last_kernel, [SMEM] + [VMEM] * 7,
        jax.ShapeDtypeStruct(whole, jnp.float32), HBM,
        [POOL, pltpu.VMEM(POST.shape, jnp.float32), pltpu.VMEM(whole, jnp.float32),
         pltpu.SemaphoreType.DMA((POPS,))],
        bytes_accessed=2 * size,
    )(receives, post, inside(post), own, *came)
    out = out.reshape(POPS, ROWS, BLK_DEV, 128).transpose(2, 0, 1, 3)
    return out.reshape(pdfs.shape)


def solution(mesh):
    placed = (P("blocks", None, None), P("blocks"), P("blocks", None), P("blocks", None))
    return jax.shard_map(
        body, mesh=mesh, in_specs=placed, out_specs=P("blocks", None, None), check_vma=False
    )
```
